256 devices in a mesh: blk: 16 (over x_lo, y, core), rep: 16 (over x_hi, z).
Axes of the slice: x: 4 (x_hi: 2, x_lo: 2; x = x_hi * 2 + x_lo), y: 4, z: 8, core: 2. Of those that a mesh axis runs over, the one named last changes fastest.
Arguments:
- features: bfloat16 [65536, 256], P(('blk', 'rep')), may hold values from -6 to 6
- tiles: bfloat16 [256, 16, 16, 128, 128], P(('blk', 'rep'))
- tile_rows: int32 [256, 16, 16], P(('blk', 'rep')), may hold values from 0 to 31
- tile_cols: int32 [256, 16, 16], P(('blk', 'rep')), may hold values from 0 to 1
- tile_counts: int32 [256, 16], P(('blk', 'rep')), may hold values from 0 to 16, as said below
- self_weight: bfloat16 [256, 256], replicated, may hold values from -0.375 to 0.375
- neigh_weight: bfloat16 [256, 256], replicated, may hold values from -0.375 to 0.375
- bias: float32 [256], replicated, may hold values from -3 to 3
- out_grad: bfloat16 [65536, 256], P(('blk', 'rep')), may hold values from -6 to 6
Outputs:
- output: bfloat16 [65536, 256], P(('blk', 'rep'))
- grad_features: bfloat16 [65536, 256], P(('blk', 'rep'))
- grad_self: float32 [256, 256], replicated
- grad_neigh: float32 [256, 256], replicated
- grad_bias: float32 [256], replicated
The draws below stay inside these ranges and needn't reach their ends.
Inputs may be any that keep to these rules, and one draw needn't show every extreme that they name: `tile_counts`: in every draw one device has all 16 slots live for every source block; other devices carry skewed loads.
All inputs are finite; a program needn't handle non-finite values.
Results may differ from the reference program's by a relative error of at most 0.0075.
Values may be sent and summed in bfloat16 or wider, within the bound.
A program may use at most 64 MiB of HBM per device.

```python
import jax
import jax.numpy as jnp
from jax import lax

D = 256
TILE = 128
ROWS = 256
SLOTS = 16
NODES = 65536
N_BLK = 16
N_REP = 16
DEVICES = 256


def draw_tiles(key, part):
    key = jax.random.fold_in(key, 11)
    first, second = jax.random.split(key)
    shape = (DEVICES, N_BLK, SLOTS, TILE, TILE)
    present = jax.random.bernoulli(first, 0.25, shape).astype(jnp.float32)
    values = jax.random.uniform(second, shape, jnp.float32, 0.5, 1.5)
    terms = max(1.0, 0.08 * N_BLK * SLOTS * TILE * TILE / ROWS)
    return (present * values * terms ** (-0.5)).astype(jnp.bfloat16)


def draw_tile_counts(key, part):
    key = jax.random.fold_in(key, 23)
    first, second, third = jax.random.split(key, 3)
    base = jax.random.randint(first, (DEVICES, N_BLK), 1, SLOTS + 1)
    heavy = jax.random.randint(second, (DEVICES, 1), 0, 4)
    counts = base * (heavy + 1) // 4
    fullest = jax.random.randint(third, (), 0, DEVICES)
    counts = jnp.where(jnp.arange(DEVICES)[:, None] == fullest, SLOTS, counts)
    return counts.astype(jnp.int32)


def touch_ends(entries, rng, least, top_value):
    extent = entries.shape
    index_at = [jax.random.randint(jax.random.fold_in(rng, axis), (), 0, extent[axis]) for axis in range(len(extent))]
    entries = entries.at[tuple(index_at)].set(least)
    longest = extent.index(max(extent))
    index_at[longest] = (index_at[longest] + 1) % extent[longest]
    return entries.at[tuple(index_at)].set(top_value)


def levels(key, shape, cuts, low, high):
    def one(dim, parts):
        draws = jax.random.uniform(jax.random.fold_in(jax.random.fold_in(key, 6), dim), (parts,), jnp.float32, low / len(cuts), high / len(cuts))
        return jnp.repeat(jnp.exp(draws), shape[dim] // parts).reshape((-1,) + (1,) * (len(shape) - dim - 1))

    level = one(*cuts[0])
    for cut in cuts[1:]:
        level = level * one(*cut)
    return level


def bell_draw(rng, extent, scale, reach, shards=(), kind=jnp.bfloat16):
    array = scale * jax.random.normal(rng, extent, jnp.float32)
    if shards:
        array = array * levels(rng, extent, shards, -0.22, 0.18)
    return jnp.clip(array, -reach, reach).astype(kind)


def setup_inputs(seed: int = 0) -> dict:
    arg_keys = jax.random.split(jax.random.key(seed), 10)
    features = bell_draw(arg_keys[0], (NODES, D), 1.0, 6.0, ((0, 256),))
    tiles = draw_tiles(jax.random.fold_in(arg_keys[9], 71), 0)
    tile_rows = touch_ends(jax.random.randint(arg_keys[2], (DEVICES, N_BLK, SLOTS), 0, N_REP * ROWS // TILE), jax.random.fold_in(arg_keys[2], 1), 0, (N_REP * ROWS // TILE) - 1).astype(jnp.int32)
    tile_cols = touch_ends(jax.random.randint(arg_keys[3], (DEVICES, N_BLK, SLOTS), 0, ROWS // TILE), jax.random.fold_in(arg_keys[3], 1), 0, (ROWS // TILE) - 1).astype(jnp.int32)
    tile_counts = draw_tile_counts(jax.random.fold_in(arg_keys[9], 71), 0)
    self_weight = bell_draw(arg_keys[5], (D, D), D ** -0.5, 0.375)
    neigh_weight = bell_draw(arg_keys[6], (D, D), D ** -0.5, 0.375)
    bias = bell_draw(arg_keys[7], (D,), 0.5, 3.0, (), jnp.float32)
    out_grad = bell_draw(arg_keys[8], (NODES, D), 1.0, 6.0, ((0, 256),))
    return dict(features=features, tiles=tiles, tile_rows=tile_rows, tile_cols=tile_cols, tile_counts=tile_counts, self_weight=self_weight, neigh_weight=neigh_weight, bias=bias, out_grad=out_grad)


def reference(features, tiles, tile_rows, tile_cols, tile_counts, self_weight, neigh_weight, bias, out_grad):
    row_tiles = ROWS // TILE
    block_tiles = N_REP * row_tiles
    feat = features.reshape(N_BLK, N_REP, row_tiles, TILE, D)
    tiles_all = tiles.reshape(N_BLK, N_REP, N_BLK, SLOTS, TILE, TILE)
    rows_all = tile_rows.reshape(N_BLK, N_REP, N_BLK, SLOTS)
    cols_all = tile_cols.reshape(N_BLK, N_REP, N_BLK, SLOTS)
    live_all = (jnp.arange(SLOTS, dtype=jnp.int32)[None, None, None, :]
                < tile_counts.reshape(N_BLK, N_REP, N_BLK)[..., None]).astype(jnp.float32)
    columns = jnp.arange(N_BLK, dtype=jnp.int32)[:, None]

    def forward_block(block):
        def add_rep(rep, total):
            source = feat[:, rep]
            picked = source[columns, cols_all[block, rep]]
            product = jnp.einsum('csij,csjd->csid', tiles_all[block, rep].astype(jnp.float32),
                                 picked.astype(jnp.float32))
            product = product * live_all[block, rep][:, :, None, None]
            return total.at[rows_all[block, rep].reshape(-1)].add(product.reshape(-1, TILE, D))
        return lax.fori_loop(0, N_REP, add_rep, jnp.zeros((block_tiles, TILE, D), jnp.float32))

    aggregate = lax.map(forward_block, jnp.arange(N_BLK, dtype=jnp.int32)).reshape(NODES, D)
    agg_low = aggregate.astype(jnp.bfloat16)
    preact = (jnp.dot(features, self_weight, preferred_element_type=jnp.float32)
              + jnp.dot(agg_low, neigh_weight, preferred_element_type=jnp.float32) + bias)
    output = (preact * jax.nn.sigmoid(preact)).astype(jnp.bfloat16)
    sigmoid_pre = jax.nn.sigmoid(preact)
    dpre = (out_grad.astype(jnp.float32) * sigmoid_pre * (1.0 + preact * (1.0 - sigmoid_pre))).astype(jnp.bfloat16)
    grad_self = jnp.einsum('nd,ne->de', features, dpre, preferred_element_type=jnp.float32)
    grad_neigh = jnp.einsum('nd,ne->de', agg_low, dpre, preferred_element_type=jnp.float32)
    grad_bias = jnp.sum(dpre.astype(jnp.float32), axis=0)
    dagg = jnp.einsum('ne,de->nd', dpre, neigh_weight, preferred_element_type=jnp.float32).astype(jnp.bfloat16)
    spread = dagg.reshape(N_BLK, block_tiles, TILE, D)

    def backward_block(block, total):
        def add_rep(rep, total):
            picked = spread[block][rows_all[block, rep]]
            product = jnp.einsum('csji,csjd->csid', tiles_all[block, rep].astype(jnp.float32),
                                 picked.astype(jnp.float32))
            product = product * live_all[block, rep][:, :, None, None]
            part = jnp.zeros((N_BLK, row_tiles, TILE, D), jnp.float32).at[columns, cols_all[block, rep]].add(product)
            return total.at[:, rep].add(part)
        return lax.fori_loop(0, N_REP, add_rep, total)

    neighbor = lax.fori_loop(0, N_BLK, backward_block,
                             jnp.zeros((N_BLK, N_REP, row_tiles, TILE, D), jnp.float32)).reshape(NODES, D)
    grad_features = (jnp.einsum('ne,de->nd', dpre, self_weight, preferred_element_type=jnp.float32)
                     + neighbor).astype(jnp.bfloat16)
    return output, grad_features, grad_self, grad_neigh, grad_bias
```

```python
import types

import jax
import jax.numpy as jnp
from jax import lax
from jax.experimental import pallas as pl
from jax.experimental.pallas import tpu as pltpu
from jax.sharding import PartitionSpec as P

BF, F32, I32 = jnp.bfloat16, jnp.float32, jnp.int32
MESH = pl.DeviceIdType.MESH
N_SRC = 16
SLOTS = 16
LIVE = N_SRC * SLOTS
TILE = 128
D = 256
SEGMENTS = 32
PAIRS = (LIVE + SEGMENTS) // 2
DEAD = 40
FWD_STEP = 24


def iota(shape, dim):
    return lax.broadcasted_iota(I32, shape, dim)


def ones_where(cond):
    return jnp.where(cond, 1.0, 0.0).astype(BF)


def dot(a, b, contract=((1,), (0,))):
    return lax.dot_general(a, b, (contract, ((), ())), preferred_element_type=F32)


def spread(table):
    slot = iota((LIVE, SLOTS), 0)
    picked = dot(ones_where(slot // SLOTS == iota((LIVE, SLOTS), 1)), table.astype(F32).astype(BF))
    own = jnp.where(slot % SLOTS == iota((LIVE, SLOTS), 1), picked, 0.0).astype(BF)
    ones = jnp.ones((LIVE, SLOTS), BF)
    return dot(own, ones, ((1,), (1,))), dot(ones, own, ((1,), (1,)))


def pair_table(key, other, by_source):
    down, along = spread(key)
    _, other_along = spread(other)
    before = (down == along) & (iota((LIVE, LIVE), 1) < iota((LIVE, LIVE), 0))
    place_in = dot(ones_where(before), jnp.ones((LIVE, 128), BF))
    member = down[:, :128] == iota((LIVE, 128), 1).astype(F32)
    size = dot(jnp.ones((LIVE, LIVE), BF), ones_where(member))
    pairs = jnp.floor((size + 1.0) * 0.5)
    group, later = iota((128, 128), 0), iota((128, 128), 1)
    if by_source:
        first_pair = dot(pairs.astype(BF), ones_where((later % 2 == 1) & (group == later - 1)))
        first_pair = first_pair + (9 * (iota((LIVE, 128), 1) // 2)).astype(F32)
    else:
        first_pair = dot(pairs.astype(BF), ones_where(group < later))
    own_first = dot(jnp.where(member & (iota((LIVE, 128), 1) < SEGMENTS), first_pair, 0.0).astype(BF), jnp.ones((128, 128), BF))
    place = 2.0 * own_first + place_in
    place = jnp.where(down[:, :128] < float(SEGMENTS), place, -1.0)
    place3 = jnp.concatenate([place, place, place], axis=1)
    place_in3 = jnp.concatenate([place_in, place_in, place_in], axis=1)
    held = place3 == iota((LIVE, 384), 1).astype(F32)
    held_low = ones_where(held)
    slot = iota((8, LIVE), 1)
    which = dot((slot - LIVE).astype(F32).astype(BF), held_low) + float(LIVE)
    what = dot(other_along[0:8].astype(BF), held_low)
    opens = dot(jnp.ones((8, LIVE), BF), ones_where(held & (place_in3 == 0.0)))
    row = iota((8, 384), 0)
    table = jnp.where(row == 0, which, jnp.where(row == 1, what, opens)).astype(I32)
    last = jnp.where(size > 0.0, first_pair + pairs, 0.0)[0:8].astype(I32)
    return table, last


def make_tables(rows, cols, counts, forward, forward_last, backward, backward_last):
    diagonal = iota((N_SRC, SLOTS), 0) == iota((N_SRC, SLOTS), 1)
    counted = jnp.where(diagonal, counts.astype(F32), 0.0).astype(BF)
    live = iota((N_SRC, SLOTS), 1).astype(F32) < dot(counted, jnp.ones((N_SRC, SLOTS), BF))
    source = 2 * iota((N_SRC, SLOTS), 0) + cols
    table, last = pair_table(jnp.where(live, rows, DEAD), source, False)
    forward[...] = table
    forward_last[...] = last
    table, last = pair_table(jnp.where(live, source, DEAD), rows, True)
    backward[...] = table
    backward_last[...] = last


def within(index, top):
    return jnp.minimum(jnp.maximum(index, 0), top)


def add_pairs(table, tiles, values, runs, first, count, running, transposed):
    for step in range(count):
        p = first + step
        left, right = within(table[0, 2 * p], LIVE), within(table[0, 2 * p + 1], LIVE)
        pick, pick_right = within(table[1, 2 * p], SEGMENTS - 1), within(table[1, 2 * p + 1], SEGMENTS - 1)
        held = jnp.concatenate([values[pick], values[pick_right]], axis=0)
        if transposed:
            product = dot(jnp.concatenate([tiles[left], tiles[right]], axis=0), held, ((0,), (0,)))
        else:
            product = dot(jnp.concatenate([tiles[left], tiles[right]], axis=1), held)
        running = product + jnp.where(table[2, 2 * p] > 0, 0.0, running)
        runs[p + 1] = running


class Wires:
    def __init__(self, send_sem, recv_sem, anyone):
        self.send_sem, self.recv_sem, self.anyone = send_sem, recv_sem, anyone
        self.names, self.pending = {}, []

    def copy(self, name, source, target, device):
        k = self.names.setdefault(name, len(self.names))
        return pltpu.make_async_remote_copy(
            src_ref=source, dst_ref=target, send_sem=self.send_sem.at[k], recv_sem=self.recv_sem.at[k],
            device_id=device, device_id_type=MESH)

    def push(self, name, source, target, device):
        copy = self.copy(name, source, target, device)
        copy.start()
        self.pending.append(copy)

    def take(self, name, target):
        self.copy(name, target, target, self.anyone).wait_recv()

    def flush(self):
        for copy in self.pending:
            copy.wait_send()
        self.pending = []


SCRATCH = dict(
    tiles=((LIVE + 1, TILE, TILE), BF), feats=((32, TILE, D), BF), runs=((PAIRS + 1, TILE, D), F32),
    daggs=((32, TILE, D), BF),
    fwd_v=((8, 384), I32), fwd_last_v=((8, 128), I32), bwd_v=((8, 384), I32), bwd_last_v=((8, 128), I32),
    self_part=((2, TILE, D), F32), aggs=((2, TILE, D), BF), dpres=((2, TILE, D), BF), base=((2, TILE, D), F32),
    a_up_out=((4, 2, TILE, D), BF), a_up_in=((4, 2, TILE, D), BF), a_down_out=((4, 2, TILE, D), BF), a_down_in=((4, 2, TILE, D), BF),
    b_up_out=((4, TILE, D), BF), b_up_in=((4, TILE, D), BF), b_down_out=((4, TILE, D), BF), b_down_in=((4, TILE, D), BF),
    bx_out=((8, TILE, D), BF), bx_in=((8, TILE, D), BF), ax_out=((TILE, D), BF), ax_in=((TILE, D), BF), a_own=((TILE, D), F32),
    core_out=((4, 2, 2, TILE, D), BF), core_in=((4, 2, 2, TILE, D), BF),
    y0_out=((2, 2, TILE, D), BF), y0_in=((2, 2, TILE, D), BF), y1_out=((2, 2, 2, TILE, D), BF), y1_in=((2, 2, 2, TILE, D), BF),
    rows=((1, N_SRC, SLOTS), I32), cols=((1, N_SRC, SLOTS), I32), counts=((1, N_SRC), I32), self_w=((D, D), BF), neigh_w=((D, D), BF),
    bias=((D,), F32), out_grad=((2 * TILE, D), BF), output=((2 * TILE, D), BF), grad_features=((2 * TILE, D), BF), grad_bias=((D,), F32),
    x_out=((2, TILE, D), BF), x_in=((2, TILE, D), BF),
    grads=((2, D, D), F32), grads_in=((D, D), F32), chip=((D, D), F32), quarter=((64, D), F32), y_parts=((3, 64, D), F32),
    x_parts=((3, 16, D), F32), z_parts=((8, 16, D), F32), full=((2, D, D), F32),
    bias_core=((2, 8, D), F32), bias_y=((4, 8, D), F32), bias_x=((4, 8, D), F32), bias_z=((8, 8, D), F32),
)
WIRES = 160


def layer_kernel(features, tiles_hbm, *rest):
    in_hbm, out_hbm, scratch = rest[:7], rest[7:12], rest[12:]
    s = types.SimpleNamespace(**dict(zip(SCRATCH, scratch)))
    fwd, fwd_last, bwd, bwd_last, send_sem, recv_sem, tile_sem, table_sem, in_sem, out_sem = scratch[len(SCRATCH):]
    tiles, feats, runs, daggs = s.tiles, s.feats, s.runs, s.daggs
    b, r = lax.axis_index("blk"), lax.axis_index("rep")
    xl, y, core = b // 8, lax.rem(b // 2, 4), lax.rem(b, 2)
    xh, z = r // 8, lax.rem(r, 8)
    x = 2 * xh + xl

    def block(xl, y, core):
        return xl * 8 + y * 2 + core

    def y_at(o):
        return lax.rem(y + o, 4)

    def z_at(o):
        return lax.rem(z + o, 8)

    def x_at(o):
        return lax.rem(x + o, 4)

    x_side, y_up, y_down, mate = (block(1 - xl, y, core), r), (block(xl, y_at(1), core), r), (block(xl, y_at(3), core), r), (block(xl, y, 1 - core), r)
    z_up, z_down, x_far = (b, xh * 8 + z_at(1)), (b, xh * 8 + z_at(7)), (b, (1 - xh) * 8 + z)
    y_peer = {o: (block(xl, y_at(o), core), r) for o in (1, 2, 3)}
    x_peer = {o: (block(lax.rem(x_at(o), 2), y, core), (x_at(o) // 2) * 8 + z) for o in (1, 2, 3)}
    z_peer = {o: (b, xh * 8 + z_at(o)) for o in range(1, 8)}
    w = Wires(send_sem, recv_sem, mate)

    load = pltpu.make_async_copy(tiles_hbm.at[0], tiles.at[pl.ds(0, LIVE)], tile_sem)
    held = (s.rows, s.cols, s.counts, s.self_w, s.neigh_w, s.bias, s.out_grad)
    reads = [pltpu.make_async_copy(features.at[pl.ds(half * TILE, TILE)], feats.at[2 * b + half], in_sem.at[half]) for half in range(2)]
    reads += [pltpu.make_async_copy(source, target, in_sem.at[2 + k]) for k, (source, target) in enumerate(zip(in_hbm, held))]
    barrier = pltpu.get_barrier_semaphore()
    partners = [mate, *y_peer.values(), *x_peer.values(), *z_peer.values()]
    for partner in partners:
        pl.semaphore_signal(barrier, inc=1, device_id=partner, device_id_type=MESH)
    for read in reads:
        read.start()
    load.start()
    rows, cols, counts, self_w, neigh_w, bias, out_grad = held
    output, grad_features, full = s.output, s.grad_features, s.full
    made = (output, grad_features, full.at[0], full.at[1], s.grad_bias)
    writes = [pltpu.make_async_copy(source, target, out_sem.at[k]) for k, (source, target) in enumerate(zip(made, out_hbm))]
    tiles[LIVE] = jnp.zeros((TILE, TILE), BF)
    runs[0] = jnp.zeros((TILE, D), F32)
    pl.semaphore_wait(barrier, len(partners))

    def feat(xl, y, core, half):
        return feats.at[2 * block(xl, y, core) + half]

    mates = []

    def spread_feat(name, where, device):
        w.push(name, feat(*where), feat(*where), device)

    def to_mate(xl, y, half):
        spread_feat("m%d" % len(mates), (xl, y, core, half), mate)
        mates.append((xl, y, half))

    def arrived(name, xl, y, half):
        w.take(name, feat(xl, y, core, half))
        to_mate(xl, y, half)

    other, before, behind, across = 1 - xl, y_at(3), y_at(1), y_at(2)
    for half in range(2):
        here = features.at[pl.ds(half * TILE, TILE)]
        there = feat(xl, y, core, half)
        w.push("fx%d" % half, here, there, x_side)
        w.push("fu0%d" % half, here, there, y_up)
        w.push("fd0%d" % half, here, there, y_down)
        w.push("m%d" % half, here, there, mate)
        mates.append((xl, y, half))

    for read in reads:
        read.wait()
    arrived("fx0", other, y, 0)
    spread_feat("fu10", (other, y, core, 0), y_up)
    spread_feat("fd10", (other, y, core, 0), y_down)
    arrived("fu00", xl, before, 0)
    spread_feat("fu2", (xl, before, core, 0), y_up)
    arrived("fx1", other, y, 1)
    spread_feat("fu11", (other, y, core, 1), y_up)
    spread_feat("fd11", (other, y, core, 1), y_down)
    arrived("fd01", xl, behind, 1)
    spread_feat("fd2", (xl, behind, core, 1), y_down)
    arrived("fd00", xl, behind, 0)
    arrived("fu01", xl, before, 1)
    arrived("fu10", other, before, 0)
    spread_feat("fu3", (other, before, core, 0), y_up)
    arrived("fd10", other, behind, 0)
    arrived("fd11", other, behind, 1)
    spread_feat("fd3", (other, behind, core, 1), y_down)
    arrived("fu11", other, before, 1)
    arrived("fu2", xl, across, 0)
    arrived("fd2", xl, across, 1)
    make_tables(rows[0], cols[0], counts[...], s.fwd_v, s.fwd_last_v, s.bwd_v, s.bwd_last_v)
    tables = [(s.fwd_v, fwd), (s.fwd_last_v, fwd_last), (s.bwd_v, bwd), (s.bwd_last_v, bwd_last)]
    tables = [pltpu.make_async_copy(here, there, table_sem.at[k]) for k, (here, there) in enumerate(tables)]
    for copy in tables:
        copy.start()
    for half in range(2):
        s.self_part[half] = dot(feats[2 * b + half], self_w[...]) + bias[...].reshape(1, D)
    arrived("fu3", other, across, 0)
    arrived("fd3", other, across, 1)
    for k, (side, at, half) in enumerate(mates):
        w.take("m%d" % k, feat(side, at, 1 - core, half))

    for copy in tables:
        copy.wait()
    load.wait()

    @pl.loop(0, PAIRS // FWD_STEP)
    def _(k):
        add_pairs(fwd, tiles, feats, runs, FWD_STEP * k, FWD_STEP, runs[FWD_STEP * k], False)

    def part(xh, z, half):
        return runs[within(fwd_last[0, (xh * 8 + z) * 2 + half], PAIRS)]

    a_up_out, a_up_in, a_down_out, a_down_in = s.a_up_out, s.a_up_in, s.a_down_out, s.a_down_in
    b_up_out, b_up_in, b_down_out, b_down_in = s.b_up_out, s.b_up_in, s.b_down_out, s.b_down_in
    bx_out, bx_in = s.bx_out, s.bx_in
    a_up_out[0, 0] = part(0, z_at(4), 0).astype(BF)
    w.push("au00", a_up_out.at[0, 0], a_up_in.at[0, 0], z_up)
    a_down_out[0, 1] = part(1, z_at(4), 0).astype(BF)
    w.push("ad01", a_down_out.at[0, 1], a_down_in.at[0, 1], z_down)
    offsets = (4, 3, 5, 2, 6, 1, 7, 0)

    def bx_send(j):
        bx_out[j] = part(1 - xh, z_at(offsets[j]), 1).astype(BF)
        w.push("bx%d" % j, bx_out.at[j], bx_in.at[j], x_far)

    bx_send(0)
    bx_send(1)
    a_up_out[1, 1] = part(1, z_at(3), 0).astype(BF)
    w.push("au11", a_up_out.at[1, 1], a_up_in.at[1, 1], z_up)
    a_down_out[1, 0] = part(0, z_at(5), 0).astype(BF)
    w.push("ad10", a_down_out.at[1, 0], a_down_in.at[1, 0], z_down)
    for j in range(2, 8):
        bx_send(j)
    low, high = pl.ds(0, TILE // 2), pl.ds(TILE // 2, TILE // 2)

    def a_step(k):
        for turn in ((0,) if k == 1 else (1, 0)):
            for name, out, into, device, o, half in (("au", a_up_out, a_up_in, z_up, 4 - k, 0), ("ad", a_down_out, a_down_in, z_down, 4 + k, 1)):
                side = half if turn == 0 else 1 - half
                w.take("%s%d%d" % (name, k - 1, side), into.at[k - 1, side])
                out[k, side] = (part(side, z_at(o), 0) + into[k - 1, side].astype(F32)).astype(BF)
                w.push("%s%d%d" % (name, k, side), out.at[k, side], into.at[k, side], device)

    def b_step(k):
        if k == 0:
            w.take("bx0", bx_in.at[0])
            value = (part(xh, z_at(4), 1) + bx_in[0].astype(F32)).astype(BF)
            b_up_out[0] = value
            b_down_out[0] = value
            w.push("bu0", b_up_out.at[0, low], b_up_in.at[0, low], z_up)
            w.push("bd0", b_down_out.at[0, high], b_down_in.at[0, high], z_down)
            return
        for name, out, into, device, j, rows_in in (("bu", b_up_out, b_up_in, z_up, 2 * k - 1, low), ("bd", b_down_out, b_down_in, z_down, 2 * k, high)):
            w.take("bx%d" % j, bx_in.at[j])
            w.take("%s%d" % (name, k - 1), into.at[0, rows_in] if k == 1 else into.at[k - 1])
            value = part(xh, z_at(offsets[j]), 1) + bx_in[j].astype(F32)
            if k > 1:
                value = value + into[k - 1].astype(F32)
            elif name == "bu":
                value = jnp.concatenate([value[:TILE // 2] + into[0, :TILE // 2].astype(F32), value[TILE // 2:]], axis=0)
            else:
                value = jnp.concatenate([value[:TILE // 2], value[TILE // 2:] + into[0, TILE // 2:].astype(F32)], axis=0)
            out[k] = value.astype(BF)
            w.push("%s%d" % (name, k), out.at[k], into.at[k], device)

    for k in (1, 2, 3):
        a_step(k)
        b_step(k - 1)
    for side in range(2):
        w.take("au3%d" % side, a_up_in.at[3, side])
        w.take("ad3%d" % side, a_down_in.at[3, side])

    def a_sum(side):
        return part(side, z, 0) + a_up_in[3, side].astype(F32) + a_down_in[3, side].astype(F32)

    s.ax_out[...] = a_sum(1 - xh).astype(BF)
    w.push("ax", s.ax_out, s.ax_in, x_far)
    b_step(3)
    s.a_own[...] = a_sum(xh)

    def layer(half, aggregate):
        here = slice(half * TILE, half * TILE + TILE)
        low_agg = aggregate.astype(BF)
        s.aggs[half] = low_agg
        preact = s.self_part[half] + dot(low_agg, neigh_w[...])
        gate = jax.nn.sigmoid(preact)
        output[here] = (preact * gate).astype(BF)
        dpre = (out_grad[here].astype(F32) * gate * (1.0 + preact * (1.0 - gate))).astype(BF)
        s.dpres[half] = dpre
        daggs[2 * r + half] = dot(dpre, neigh_w[...], ((1,), (1,))).astype(BF)

    def dagg(xh, z, half, rows=None):
        at = (xh * 8 + z) * 2 + half
        return daggs.at[at] if rows is None else daggs.at[at, rows]

    def spread_dagg(name, where, device, rows=None):
        w.push(name, dagg(*where, rows), dagg(*where, rows), device)

    w.take("ax", s.ax_in)
    layer(0, s.a_own[...] + s.ax_in[...].astype(F32))
    spread_dagg("gu1", (xh, z, 0), z_up)
    spread_dagg("gd1", (xh, z, 0), z_down)
    spread_dagg("x0", (xh, z, 0), x_far)
    w.take("bx7", bx_in.at[7])
    w.take("bu3", b_up_in.at[3])
    w.take("bd3", b_down_in.at[3])
    layer(1, part(xh, z, 1) + bx_in[7].astype(F32) + b_up_in[3].astype(F32) + b_down_in[3].astype(F32))
    spread_dagg("gx", (xh, z, 1), x_far)
    spread_dagg("hu1", (xh, z, 1), z_up)
    spread_dagg("hd1", (xh, z, 1), z_down)

    writes[0].start()
    aggs, dpres, grads = s.aggs, s.dpres, s.grads
    w.take("gx", dagg(1 - xh, z, 1))
    spread_dagg("iu1", (1 - xh, z, 1), z_up)
    spread_dagg("id1", (1 - xh, z, 1), z_down)

    def gather_step(k):
        for name, side, half in (("g", xh, 0), ("h", xh, 1), ("i", 1 - xh, 1)):
            for way, device, o, rows in (("u", z_up, 8 - k, low), ("d", z_down, k, high)):
                rows_in = rows if k == 4 else None
                w.take("%s%s%d" % (name, way, k), dagg(side, z_at(o), half, rows_in))
                if k < 4:
                    spread_dagg("%s%s%d" % (name, way, k + 1), (side, z_at(o), half), device, rows if k == 3 else None)
                if half == 0:
                    spread_dagg("x%s%d" % (way, k), (side, z_at(o), half), x_far, rows_in)

    quarter, chip, z_parts = s.quarter, s.chip, s.z_parts

    def weights_y():
        w.take("wc", s.grads_in)
        w.take("vc", bias_core.at[1])
        chip[...] = grads[core] + s.grads_in[...]
        bias_y[y] = bias_core[0] + bias_core[1]
        for o in (1, 2, 3):
            w.push("wy%d" % o, chip.at[pl.ds(64 * y_at(o), 64)], s.y_parts.at[o - 1], y_peer[o])
            w.push("vy%d" % o, bias_y.at[y], bias_y.at[y], y_peer[o])

    def weights_x():
        for o in (1, 2, 3):
            w.take("wy%d" % o, s.y_parts.at[o - 1])
            w.take("vy%d" % o, bias_y.at[y_at(4 - o)])
        quarter[...] = chip[pl.ds(64 * y, 64)] + s.y_parts[0] + s.y_parts[1] + s.y_parts[2]
        bias_x[x] = (bias_y[0] + bias_y[1]) + (bias_y[2] + bias_y[3])
        for o in (1, 2, 3):
            w.push("wx%d" % o, quarter.at[pl.ds(16 * x_at(o), 16)], s.x_parts.at[o - 1], x_peer[o])
            w.push("vx%d" % o, bias_x.at[x], bias_x.at[x], x_peer[o])

    def weights_z():
        for o in (1, 2, 3):
            w.take("wx%d" % o, s.x_parts.at[o - 1])
            w.take("vx%d" % o, bias_x.at[x_at(4 - o)])
        z_parts[z] = quarter[pl.ds(16 * x, 16)] + s.x_parts[0] + s.x_parts[1] + s.x_parts[2]
        bias_z[z] = (bias_x[0] + bias_x[1]) + (bias_x[2] + bias_x[3])
        for o in range(1, 8):
            w.push("wz%d" % o, z_parts.at[z], z_parts.at[z], z_peer[o])
            w.push("vz%d" % o, bias_z.at[z], bias_z.at[z], z_peer[o])

    def rows_of(y, x=None):
        return full.at[core, pl.ds(64 * y, 64)] if x is None else full.at[core, pl.ds(64 * y + 16 * x, 16)]

    def weights_total():
        for o in range(1, 8):
            w.take("wz%d" % o, z_parts.at[z_at(8 - o)])
            w.take("vz%d" % o, bias_z.at[z_at(8 - o)])
        total, bias_total = z_parts[0], bias_z[0]
        for o in range(1, 8):
            total, bias_total = total + z_parts[o], bias_total + bias_z[o]
        full[core, pl.ds(64 * y + 16 * x, 16)] = total
        s.grad_bias[...] = bias_total[0]
        writes[4].start()
        for o in (1, 2, 3):
            w.push("tx%d" % o, rows_of(y, x), rows_of(y, x), x_peer[o])

    def weights_back_y():
        for o in (1, 2, 3):
            w.take("tx%d" % o, rows_of(y, x_at(4 - o)))
        for o in (1, 2, 3):
            w.push("ty%d" % o, rows_of(y), rows_of(y), y_peer[o])

    def weights_back_core():
        for o in (1, 2, 3):
            w.take("ty%d" % o, rows_of(y_at(4 - o)))
        w.push("tc", full.at[core], full.at[core], mate)

    gather_step(1)
    dpre = dpres[...].reshape(2 * TILE, D)
    grads[0] = dot(feats[pl.ds(2 * b, 2)].reshape(2 * TILE, D), dpre, ((0,), (0,)))
    grads[1] = dot(aggs[...].reshape(2 * TILE, D), dpre, ((0,), (0,)))
    w.push("wc", grads.at[1 - core], s.grads_in, mate)
    bias_core, bias_y, bias_x, bias_z = s.bias_core, s.bias_y, s.bias_x, s.bias_z
    bias_core[0] = jnp.broadcast_to(jnp.sum(dpre.astype(F32), axis=0, keepdims=True), (8, D))
    w.push("vc", bias_core.at[0], bias_core.at[1], mate)
    for half in range(2):
        s.base[half] = dot(dpres[half], self_w[...], ((1,), (1,)))
    gather_step(2)
    weights_y()
    gather_step(3)
    weights_x()
    gather_step(4)
    weights_z()
    w.take("x0", dagg(1 - xh, z, 0))
    for k in (1, 2, 3, 4):
        w.take("xu%d" % k, dagg(1 - xh, z_at(8 - k), 0, low if k == 4 else None))
        w.take("xd%d" % k, dagg(1 - xh, z_at(k), 0, high if k == 4 else None))

    core_out, core_in = s.core_out, s.core_in
    y0_out, y0_in, y1_out, y1_in = s.y0_out, s.y0_in, s.y1_out, s.y1_in
    groups = (((1, 2), (0, 2)), ((1, 1), (1, 3)), ((0, 1), (0, 3)), ((1, 0), (0, 0)))

    def column(k):
        return (xl, other)[k]

    def back(k, o, to_core):
        to = block(column(k), y_at(o), to_core)
        add_pairs(bwd, tiles, daggs, runs, 9 * to, 9, jnp.zeros((TILE, D), F32), True)

    def term(k, o, to_core, half):
        return runs[within(bwd_last[0, 2 * block(column(k), y_at(o), to_core) + half], PAIRS)]

    def for_mate(g):
        for j, (k, o) in enumerate(groups[g]):
            back(k, o, 1 - core)
        for j, (k, o) in enumerate(groups[g]):
            for half in range(2):
                core_out[g, j, half] = term(k, o, 1 - core, half).astype(BF)
            w.push("k%d%d" % (g, j), core_out.at[g, j], core_in.at[g, j], mate)

    def for_own(g):
        for k, o in groups[g]:
            back(k, o, core)

    def chip_term(g, j, half):
        k, o = groups[g][j]
        return term(k, o, core, half) + core_in[g, j, half].astype(F32)

    def opposite():
        for j in range(2):
            k = groups[0][j][0]
            w.take("k0%d" % j, core_in.at[0, j])
            for way, device in enumerate((y_up, y_down)):
                y0_out[way, k] = chip_term(0, j, way).astype(BF)
                w.push("p%d%d" % (way, k), y0_out.at[way, k], y0_in.at[way, k], device)

    def neighbours(g):
        k = groups[g][0][0]
        for way, device in enumerate((y_up, y_down)):
            w.take("k%d%d" % (g, way), core_in.at[g, way])
            y1_out[way, k, 1 - way] = chip_term(g, way, 1 - way).astype(BF)
            w.push("q%d%d%d" % (way, k, 1 - way), y1_out.at[way, k, 1 - way], y1_in.at[way, k, 1 - way], device)
        for way, device in enumerate((y_up, y_down)):
            w.take("p%d%d" % (way, k), y0_in.at[way, k])
            y1_out[way, k, way] = (chip_term(g, way, way) + y0_in[way, k].astype(F32)).astype(BF)
            w.push("q%d%d%d" % (way, k, way), y1_out.at[way, k, way], y1_in.at[way, k, way], device)

    def column_sum(j, half):
        k = groups[3][j][0]
        for way in range(2):
            w.take("q%d%d%d" % (way, k, half), y1_in.at[way, k, half])
        return chip_term(3, j, half) + y1_in[0, k, half].astype(F32) + y1_in[1, k, half].astype(F32)

    for_mate(0)
    for_mate(1)
    for_own(0)
    opposite()
    weights_total()
    for_mate(2)
    for_own(1)
    neighbours(1)
    weights_back_y()
    for_mate(3)
    for_own(2)
    neighbours(2)
    weights_back_core()
    for_own(3)
    w.take("k30", core_in.at[3, 0])
    w.take("k31", core_in.at[3, 1])
    w.take("tc", full.at[1 - core])
    writes[2].start()
    writes[3].start()
    for half in range(2):
        s.x_out[half] = column_sum(0, half).astype(BF)
        w.push("x%d" % (half + 8), s.x_out.at[half], s.x_in.at[half], x_side)
    for half in range(2):
        s.base[half] = s.base[half] + column_sum(1, half)
    for half in range(2):
        w.take("x%d" % (half + 8), s.x_in.at[half])
        grad_features[half * TILE:half * TILE + TILE] = (s.base[half] + s.x_in[half].astype(F32)).astype(BF)
    writes[1].start()
    for write in writes:
        write.wait()
    w.flush()
    assert len(w.names) <= WIRES


OUTPUTS = [jax.ShapeDtypeStruct((2 * TILE, D), BF)] * 2 + [jax.ShapeDtypeStruct((D, D), F32)] * 2 + [jax.ShapeDtypeStruct((D,), F32)]


def hand_over(*refs):
    for k in range(5):
        refs[5 + k][...] = refs[k][...]


def body(features, tiles, tile_rows, tile_cols, tile_counts, self_weight, neigh_weight, bias, out_grad):
    anywhere = pl.BlockSpec(memory_space=pl.ANY)
    made = pl.pallas_call(
        layer_kernel,
        out_shape=OUTPUTS,
        in_specs=[anywhere] * 9,
        out_specs=[anywhere] * 5,
        scratch_shapes=[pltpu.VMEM(*spec) for spec in SCRATCH.values()] + [
            pltpu.SMEM((8, 384), I32), pltpu.SMEM((8, 128), I32), pltpu.SMEM((8, 384), I32), pltpu.SMEM((8, 128), I32),
            pltpu.SemaphoreType.DMA((WIRES,)), pltpu.SemaphoreType.DMA((WIRES,)),
            pltpu.SemaphoreType.DMA, pltpu.SemaphoreType.DMA((4,)), pltpu.SemaphoreType.DMA((9,)), pltpu.SemaphoreType.DMA((5,)),
        ],
        compiler_params=pltpu.CompilerParams(collective_id=0, has_side_effects=True, vmem_limit_bytes=56 << 20),
        name="sage_layer",
    )(features, tiles.reshape(1, LIVE, TILE, TILE), tile_rows, tile_cols, tile_counts, self_weight, neigh_weight, bias, out_grad)
    return pl.pallas_call(
        hand_over,
        out_shape=OUTPUTS,
        in_specs=[pl.BlockSpec(memory_space=pltpu.VMEM)] * 5,
        out_specs=[pl.BlockSpec(memory_space=pltpu.VMEM)] * 5,
        name="hand_over",
    )(*made)


def solution(mesh):
    split = ("blk", "rep")
    return jax.shard_map(
        body,
        mesh=mesh,
        in_specs=(P(split, None), P(split, None, None, None, None), P(split, None, None), P(split, None, None), P(split, None),
                  P(), P(), P(), P(split, None)),
        out_specs=(P(split, None), P(split, None), P(), P(), P()),
        check_vma=False,
    )
```

```python
import types

import jax
import jax.numpy as jnp
from jax import lax
from jax.experimental import pallas as pl
from jax.experimental.pallas import tpu as pltpu
from jax.sharding import PartitionSpec as P

BF, F32, I32 = jnp.bfloat16, jnp.float32, jnp.int32
MESH = pl.DeviceIdType.MESH
N_SRC = 16
SLOTS = 16
LIVE = N_SRC * SLOTS
TILE = 128
D = 256
SEGMENTS = 32
PAIRS = (LIVE + SEGMENTS) // 2
DEAD = 40
FWD_STEP = 48


def iota(shape, dim):
    return lax.broadcasted_iota(I32, shape, dim)


def ones_where(cond):
    return jnp.where(cond, 1.0, 0.0).astype(BF)


def dot(a, b, contract=((1,), (0,))):
    return lax.dot_general(a, b, (contract, ((), ())), preferred_element_type=F32)


def spread(table):
    slot = iota((LIVE, SLOTS), 0)
    picked = dot(ones_where(slot // SLOTS == iota((LIVE, SLOTS), 1)), table.astype(F32).astype(BF))
    own = jnp.where(slot % SLOTS == iota((LIVE, SLOTS), 1), picked, 0.0).astype(BF)
    ones = jnp.ones((LIVE, SLOTS), BF)
    return dot(own, ones, ((1,), (1,))), dot(ones, own, ((1,), (1,)))


def pair_table(key, other, by_source):
    down, along = spread(key)
    _, other_along = spread(other)
    before = (down == along) & (iota((LIVE, LIVE), 1) < iota((LIVE, LIVE), 0))
    place_in = dot(ones_where(before), jnp.ones((LIVE, 128), BF))
    member = down[:, :128] == iota((LIVE, 128), 1).astype(F32)
    size = dot(jnp.ones((LIVE, LIVE), BF), ones_where(member))
    pairs = jnp.floor((size + 1.0) * 0.5)
    group, later = iota((128, 128), 0), iota((128, 128), 1)
    if by_source:
        first_pair = dot(pairs.astype(BF), ones_where((later % 2 == 1) & (group == later - 1)))
        first_pair = first_pair + (9 * (iota((LIVE, 128), 1) // 2)).astype(F32)
    else:
        first_pair = dot(pairs.astype(BF), ones_where(group < later))
    own_first = dot(jnp.where(member & (iota((LIVE, 128), 1) < SEGMENTS), first_pair, 0.0).astype(BF), jnp.ones((128, 128), BF))
    place = 2.0 * own_first + place_in
    place = jnp.where(down[:, :128] < float(SEGMENTS), place, -1.0)
    place3 = jnp.concatenate([place, place, place], axis=1)
    place_in3 = jnp.concatenate([place_in, place_in, place_in], axis=1)
    held = place3 == iota((LIVE, 384), 1).astype(F32)
    held_low = ones_where(held)
    slot = iota((8, LIVE), 1)
    which = dot((slot - LIVE).astype(F32).astype(BF), held_low) + float(LIVE)
    what = dot(other_along[0:8].astype(BF), held_low)
    opens = dot(jnp.ones((8, LIVE), BF), ones_where(held & (place_in3 == 0.0)))
    row = iota((8, 384), 0)
    table = jnp.where(row == 0, which, jnp.where(row == 1, what, opens)).astype(I32)
    last = jnp.where(size > 0.0, first_pair + pairs, 0.0)[0:8].astype(I32)
    return table, last


def make_tables(rows, cols, counts, forward, forward_last, backward, backward_last):
    diagonal = iota((N_SRC, SLOTS), 0) == iota((N_SRC, SLOTS), 1)
    counted = jnp.where(diagonal, counts.astype(F32), 0.0).astype(BF)
    live = iota((N_SRC, SLOTS), 1).astype(F32) < dot(counted, jnp.ones((N_SRC, SLOTS), BF))
    source = 2 * iota((N_SRC, SLOTS), 0) + cols
    table, last = pair_table(jnp.where(live, rows, DEAD), source, False)
    forward[...] = table
    forward_last[...] = last
    table, last = pair_table(jnp.where(live, source, DEAD), rows, True)
    backward[...] = table
    backward_last[...] = last


def within(index, top):
    return jnp.minimum(jnp.maximum(index, 0), top)


def add_pairs(table, tiles, values, runs, first, count, running, transposed):
    for step in range(count):
        p = first + step
        left, right = within(table[0, 2 * p], LIVE), within(table[0, 2 * p + 1], LIVE)
        pick, pick_right = within(table[1, 2 * p], SEGMENTS - 1), within(table[1, 2 * p + 1], SEGMENTS - 1)
        held = jnp.concatenate([values[pick], values[pick_right]], axis=0)
        if transposed:
            product = dot(jnp.concatenate([tiles[left], tiles[right]], axis=0), held, ((0,), (0,)))
        else:
            product = dot(jnp.concatenate([tiles[left], tiles[right]], axis=1), held)
        running = product + jnp.where(table[2, 2 * p] > 0, 0.0, running)
        runs[p + 1] = running


class Wires:
    def __init__(self, send_sem, recv_sem, anyone):
        self.send_sem, self.recv_sem, self.anyone = send_sem, recv_sem, anyone
        self.names, self.pending = {}, []

    def copy(self, name, source, target, device):
        k = self.names.setdefault(name, len(self.names))
        return pltpu.make_async_remote_copy(
            src_ref=source, dst_ref=target, send_sem=self.send_sem.at[k], recv_sem=self.recv_sem.at[k],
            device_id=device, device_id_type=MESH)

    def push(self, name, source, target, device):
        copy = self.copy(name, source, target, device)
        copy.start()
        self.pending.append(copy)

    def take(self, name, target):
        self.copy(name, target, target, self.anyone).wait_recv()

    def flush(self):
        for copy in self.pending:
            copy.wait_send()
        self.pending = []


SCRATCH = dict(
    tiles=((LIVE + 1, TILE, TILE), BF), feats=((32, TILE, D), BF), runs=((PAIRS + 1, TILE, D), F32),
    daggs=((32, TILE, D), BF),
    fwd_v=((8, 384), I32), fwd_last_v=((8, 128), I32), bwd_v=((8, 384), I32), bwd_last_v=((8, 128), I32),
    self_part=((2, TILE, D), F32), aggs=((2, TILE, D), BF), dpres=((2, TILE, D), BF), base=((2, TILE, D), F32),
    a_up_out=((4, 2, TILE, D), BF), a_up_in=((4, 2, TILE, D), BF), a_down_out=((4, 2, TILE, D), BF), a_down_in=((4, 2, TILE, D), BF),
    b_up_out=((4, TILE, D), BF), b_up_in=((4, TILE, D), BF), b_down_out=((4, TILE, D), BF), b_down_in=((4, TILE, D), BF),
    bx_out=((8, TILE, D), BF), bx_in=((8, TILE, D), BF), ax_out=((TILE, D), BF), ax_in=((TILE, D), BF), a_own=((TILE, D), F32),
    core_out=((4, 2, 2, TILE, D), BF), core_in=((4, 2, 2, TILE, D), BF),
    y0_out=((2, 2, TILE, D), BF), y0_in=((2, 2, TILE, D), BF), y1_out=((2, 2, 2, TILE, D), BF), y1_in=((2, 2, 2, TILE, D), BF),
    rows=((1, N_SRC, SLOTS), I32), cols=((1, N_SRC, SLOTS), I32), counts=((1, N_SRC), I32), self_w=((D, D), BF), neigh_w=((D, D), BF),
    bias=((D,), F32), out_grad=((2 * TILE, D), BF), output=((2 * TILE, D), BF), grad_features=((2 * TILE, D), BF), grad_bias=((D,), F32),
    x_out=((2, TILE, D), BF), x_in=((2, TILE, D), BF),
    grads=((2, 4, 64, D), F32), grads_in=((4, 64, D), F32), chip=((4, 72, D), F32), y_parts=((4, 72, D), F32), quarter=((4, 24, D), F32), x_parts=((4, 24, D), F32),
    z_parts=((8, 24, D), F32), full=((2, D, D), F32), bias_core=((2, 8, D), F32),
)
WIRES = 160


def layer_kernel(features, tiles_hbm, *rest):
    in_hbm, out_hbm, scratch = rest[:7], rest[7:12], rest[12:]
    s = types.SimpleNamespace(**dict(zip(SCRATCH, scratch)))
    fwd, fwd_last, bwd, bwd_last, send_sem, recv_sem, tile_sem, table_sem, in_sem, out_sem = scratch[len(SCRATCH):]
    tiles, feats, runs, daggs = s.tiles, s.feats, s.runs, s.daggs
    b, r = lax.axis_index("blk"), lax.axis_index("rep")
    xl, y, core = b // 8, lax.rem(b // 2, 4), lax.rem(b, 2)
    xh, z = r // 8, lax.rem(r, 8)
    x = 2 * xh + xl

    def block(xl, y, core):
        return xl * 8 + y * 2 + core

    def y_at(o):
        return lax.rem(y + o, 4)

    def z_at(o):
        return lax.rem(z + o, 8)

    def x_at(o):
        return lax.rem(x + o, 4)

    x_side, y_up, y_down, mate = (block(1 - xl, y, core), r), (block(xl, y_at(1), core), r), (block(xl, y_at(3), core), r), (block(xl, y, 1 - core), r)
    z_up, z_down, x_far = (b, xh * 8 + z_at(1)), (b, xh * 8 + z_at(7)), (b, (1 - xh) * 8 + z)
    turns = [(i, j) for i in range(4) for j in range(4) if i or j]
    plane = {(i, j): (block(lax.rem(x_at(i), 2), y_at(j), core), (x_at(i) // 2) * 8 + z) for i, j in turns}

    def plane_part(i, j):
        return 4 * y_at(j) + x_at(i)

    own_part = 4 * y + x
    z_peer = {o: (b, xh * 8 + z_at(o)) for o in range(1, 8)}
    w = Wires(send_sem, recv_sem, mate)

    load = pltpu.make_async_copy(tiles_hbm.at[0], tiles.at[pl.ds(0, LIVE)], tile_sem)
    held = (s.rows, s.cols, s.counts, s.self_w, s.neigh_w, s.bias, s.out_grad)
    reads = [pltpu.make_async_copy(features.at[pl.ds(half * TILE, TILE)], feats.at[2 * b + half], in_sem.at[half]) for half in range(2)]
    reads += [pltpu.make_async_copy(source, target, in_sem.at[2 + k]) for k, (source, target) in enumerate(zip(in_hbm, held))]
    barrier = pltpu.get_barrier_semaphore()
    partners = [mate, *plane.values(), *z_peer.values()]
    for partner in partners:
        pl.semaphore_signal(barrier, inc=1, device_id=partner, device_id_type=MESH)
    for read in reads:
        read.start()
    load.start()
    rows, cols, counts, self_w, neigh_w, bias, out_grad = held
    output, grad_features, full = s.output, s.grad_features, s.full
    made = (output, grad_features, full.at[0], full.at[1], s.grad_bias)
    writes = [pltpu.make_async_copy(source, target, out_sem.at[k]) for k, (source, target) in enumerate(zip(made, out_hbm))]
    tiles[LIVE] = jnp.zeros((TILE, TILE), BF)
    runs[0] = jnp.zeros((TILE, D), F32)
    pl.semaphore_wait(barrier, len(partners))

    def feat(xl, y, core, half):
        return feats.at[2 * block(xl, y, core) + half]

    mates = []

    def spread_feat(name, where, device):
        w.push(name, feat(*where), feat(*where), device)

    def to_mate(xl, y, half):
        spread_feat("m%d" % len(mates), (xl, y, core, half), mate)
        mates.append((xl, y, half))

    def arrived(name, xl, y, half):
        w.take(name, feat(xl, y, core, half))
        to_mate(xl, y, half)

    other, before, behind, across = 1 - xl, y_at(3), y_at(1), y_at(2)
    for half in range(2):
        here = features.at[pl.ds(half * TILE, TILE)]
        there = feat(xl, y, core, half)
        w.push("fx%d" % half, here, there, x_side)
        w.push("fu0%d" % half, here, there, y_up)
        w.push("fd0%d" % half, here, there, y_down)
        w.push("m%d" % half, here, there, mate)
        mates.append((xl, y, half))

    for read in reads:
        read.wait()
    arrived("fx0", other, y, 0)
    spread_feat("fu10", (other, y, core, 0), y_up)
    spread_feat("fd10", (other, y, core, 0), y_down)
    arrived("fu00", xl, before, 0)
    spread_feat("fu2", (xl, before, core, 0), y_up)
    arrived("fx1", other, y, 1)
    spread_feat("fu11", (other, y, core, 1), y_up)
    spread_feat("fd11", (other, y, core, 1), y_down)
    arrived("fd01", xl, behind, 1)
    spread_feat("fd2", (xl, behind, core, 1), y_down)
    arrived("fd00", xl, behind, 0)
    arrived("fu01", xl, before, 1)
    arrived("fu10", other, before, 0)
    spread_feat("fu3", (other, before, core, 0), y_up)
    arrived("fd10", other, behind, 0)
    arrived("fd11", other, behind, 1)
    spread_feat("fd3", (other, behind, core, 1), y_down)
    arrived("fu11", other, before, 1)
    arrived("fu2", xl, across, 0)
    arrived("fd2", xl, across, 1)
    make_tables(rows[0], cols[0], counts[...], s.fwd_v, s.fwd_last_v, s.bwd_v, s.bwd_last_v)
    tables = [(s.fwd_v, fwd), (s.fwd_last_v, fwd_last), (s.bwd_v, bwd), (s.bwd_last_v, bwd_last)]
    tables = [pltpu.make_async_copy(here, there, table_sem.at[k]) for k, (here, there) in enumerate(tables)]
    for copy in tables:
        copy.start()
    for half in range(2):
        s.self_part[half] = dot(feats[2 * b + half], self_w[...]) + bias[...].reshape(1, D)
    arrived("fu3", other, across, 0)
    arrived("fd3", other, across, 1)
    for k, (side, at, half) in enumerate(mates):
        w.take("m%d" % k, feat(side, at, 1 - core, half))

    for copy in tables:
        copy.wait()
    load.wait()

    @pl.loop(0, PAIRS // FWD_STEP)
    def _(k):
        add_pairs(fwd, tiles, feats, runs, FWD_STEP * k, FWD_STEP, runs[FWD_STEP * k], False)

    def part(xh, z, half):
        return runs[within(fwd_last[0, (xh * 8 + z) * 2 + half], PAIRS)]

    a_up_out, a_up_in, a_down_out, a_down_in = s.a_up_out, s.a_up_in, s.a_down_out, s.a_down_in
    b_up_out, b_up_in, b_down_out, b_down_in = s.b_up_out, s.b_up_in, s.b_down_out, s.b_down_in
    bx_out, bx_in = s.bx_out, s.bx_in
    a_up_out[0, 0] = part(0, z_at(4), 0).astype(BF)
    w.push("au00", a_up_out.at[0, 0], a_up_in.at[0, 0], z_up)
    a_down_out[0, 1] = part(1, z_at(4), 0).astype(BF)
    w.push("ad01", a_down_out.at[0, 1], a_down_in.at[0, 1], z_down)
    offsets = (4, 3, 5, 2, 6, 1, 7, 0)

    def bx_send(j):
        bx_out[j] = part(1 - xh, z_at(offsets[j]), 1).astype(BF)
        w.push("bx%d" % j, bx_out.at[j], bx_in.at[j], x_far)

    bx_send(0)
    bx_send(1)
    a_up_out[1, 1] = part(1, z_at(3), 0).astype(BF)
    w.push("au11", a_up_out.at[1, 1], a_up_in.at[1, 1], z_up)
    a_down_out[1, 0] = part(0, z_at(5), 0).astype(BF)
    w.push("ad10", a_down_out.at[1, 0], a_down_in.at[1, 0], z_down)
    for j in range(2, 8):
        bx_send(j)
    low, high = pl.ds(0, TILE // 2), pl.ds(TILE // 2, TILE // 2)

    def a_step(k):
        for turn in ((0,) if k == 1 else (1, 0)):
            for name, out, into, device, o, half in (("au", a_up_out, a_up_in, z_up, 4 - k, 0), ("ad", a_down_out, a_down_in, z_down, 4 + k, 1)):
                side = half if turn == 0 else 1 - half
                w.take("%s%d%d" % (name, k - 1, side), into.at[k - 1, side])
                out[k, side] = (part(side, z_at(o), 0) + into[k - 1, side].astype(F32)).astype(BF)
                w.push("%s%d%d" % (name, k, side), out.at[k, side], into.at[k, side], device)

    def b_step(k):
        if k == 0:
            w.take("bx0", bx_in.at[0])
            value = (part(xh, z_at(4), 1) + bx_in[0].astype(F32)).astype(BF)
            b_up_out[0] = value
            b_down_out[0] = value
            w.push("bu0", b_up_out.at[0, low], b_up_in.at[0, low], z_up)
            w.push("bd0", b_down_out.at[0, high], b_down_in.at[0, high], z_down)
            return
        for name, out, into, device, j, rows_in in (("bu", b_up_out, b_up_in, z_up, 2 * k - 1, low), ("bd", b_down_out, b_down_in, z_down, 2 * k, high)):
            w.take("bx%d" % j, bx_in.at[j])
            w.take("%s%d" % (name, k - 1), into.at[0, rows_in] if k == 1 else into.at[k - 1])
            value = part(xh, z_at(offsets[j]), 1) + bx_in[j].astype(F32)
            if k > 1:
                value = value + into[k - 1].astype(F32)
            elif name == "bu":
                value = jnp.concatenate([value[:TILE // 2] + into[0, :TILE // 2].astype(F32), value[TILE // 2:]], axis=0)
            else:
                value = jnp.concatenate([value[:TILE // 2], value[TILE // 2:] + into[0, TILE // 2:].astype(F32)], axis=0)
            out[k] = value.astype(BF)
            w.push("%s%d" % (name, k), out.at[k], into.at[k], device)

    for k in (1, 2, 3):
        a_step(k)
        b_step(k - 1)
    for side in range(2):
        w.take("au3%d" % side, a_up_in.at[3, side])
        w.take("ad3%d" % side, a_down_in.at[3, side])

    def a_sum(side):
        return part(side, z, 0) + a_up_in[3, side].astype(F32) + a_down_in[3, side].astype(F32)

    s.ax_out[...] = a_sum(1 - xh).astype(BF)
    w.push("ax", s.ax_out, s.ax_in, x_far)
    b_step(3)
    s.a_own[...] = a_sum(xh)

    def layer(half, aggregate):
        here = slice(half * TILE, half * TILE + TILE)
        low_agg = aggregate.astype(BF)
        s.aggs[half] = low_agg
        preact = s.self_part[half] + dot(low_agg, neigh_w[...])
        gate = jax.nn.sigmoid(preact)
        output[here] = (preact * gate).astype(BF)
        dpre = (out_grad[here].astype(F32) * gate * (1.0 + preact * (1.0 - gate))).astype(BF)
        s.dpres[half] = dpre
        daggs[2 * r + half] = dot(dpre, neigh_w[...], ((1,), (1,))).astype(BF)

    def dagg(xh, z, half, rows=None):
        at = (xh * 8 + z) * 2 + half
        return daggs.at[at] if rows is None else daggs.at[at, rows]

    def spread_dagg(name, where, device, rows=None):
        w.push(name, dagg(*where, rows), dagg(*where, rows), device)

    w.take("ax", s.ax_in)
    layer(0, s.a_own[...] + s.ax_in[...].astype(F32))
    spread_dagg("gu1", (xh, z, 0), z_up)
    spread_dagg("gd1", (xh, z, 0), z_down)
    spread_dagg("x0", (xh, z, 0), x_far)
    w.take("bx7", bx_in.at[7])
    w.take("bu3", b_up_in.at[3])
    w.take("bd3", b_down_in.at[3])
    layer(1, part(xh, z, 1) + bx_in[7].astype(F32) + b_up_in[3].astype(F32) + b_down_in[3].astype(F32))
    spread_dagg("gx", (xh, z, 1), x_far)
    spread_dagg("hu1", (xh, z, 1), z_up)
    spread_dagg("hd1", (xh, z, 1), z_down)

    writes[0].start()
    aggs, dpres, grads = s.aggs, s.dpres, s.grads
    w.take("gx", dagg(1 - xh, z, 1))
    spread_dagg("iu1", (1 - xh, z, 1), z_up)
    spread_dagg("id1", (1 - xh, z, 1), z_down)

    def gather_step(k):
        for name, side, half in (("g", xh, 0), ("h", xh, 1), ("i", 1 - xh, 1)):
            for way, device, o, rows in (("u", z_up, 8 - k, low), ("d", z_down, k, high)):
                rows_in = rows if k == 4 else None
                w.take("%s%s%d" % (name, way, k), dagg(side, z_at(o), half, rows_in))
                if k < 4:
                    spread_dagg("%s%s%d" % (name, way, k + 1), (side, z_at(o), half), device, rows if k == 3 else None)
                if half == 0:
                    spread_dagg("x%s%d" % (way, k), (side, z_at(o), half), x_far, rows_in)

    chip, y_parts, quarter, x_parts, z_parts = s.chip, s.y_parts, s.quarter, s.x_parts, s.z_parts

    def weights_y():
        w.take("wc", s.grads_in)
        w.take("vc", bias_core.at[1])
        chip[:, 0:64] = grads[core] + s.grads_in[...]
        chip[:, 64:72] = jnp.broadcast_to((bias_core[0] + bias_core[1])[None], (4, 8, D))
        y_parts[y] = chip[y]
        for o in (1, 2, 3):
            w.push("wy%d" % o, chip.at[y_at(o)], y_parts.at[y], plane[0, o])

    def weights_x():
        for o in (1, 2, 3):
            w.take("wy%d" % o, y_parts.at[y_at(4 - o)])
        total = (y_parts[0] + y_parts[1]) + (y_parts[2] + y_parts[3])
        quarter[:, 0:16] = total[0:64].reshape(4, 16, D)
        quarter[:, 16:24] = jnp.broadcast_to(total[64:72][None], (4, 8, D))
        x_parts[x] = quarter[x]
        for o in (1, 2, 3):
            w.push("wx%d" % o, quarter.at[x_at(o)], x_parts.at[x], plane[o, 0])

    def weights_z():
        for o in (1, 2, 3):
            w.take("wx%d" % o, x_parts.at[x_at(4 - o)])
        total = (x_parts[0] + x_parts[1]) + (x_parts[2] + x_parts[3])
        z_parts[z] = total
        for o in range(1, 8):
            w.push("wz%d" % o, z_parts.at[z], z_parts.at[z], z_peer[o])

    def rows_of(part):
        return full.at[core, pl.ds(16 * part, 16)]

    def weights_total():
        for o in range(1, 8):
            w.take("wz%d" % o, z_parts.at[z_at(8 - o)])
        total = z_parts[0]
        for o in range(1, 8):
            total = total + z_parts[o]
        full[core, pl.ds(16 * own_part, 16)] = total[0:16]
        s.grad_bias[...] = total[16]
        writes[4].start()
        for i, j in turns:
            w.push("t%d%d" % (i, j), rows_of(own_part), rows_of(own_part), plane[i, j])

    def weights_back_core():
        for i, j in turns:
            w.take("t%d%d" % (i, j), rows_of(plane_part(4 - i, 4 - j)))
        w.push("tc", full.at[core], full.at[core], mate)

    gather_step(1)
    dpre = dpres[...].reshape(2 * TILE, D)
    grads[0] = dot(feats[pl.ds(2 * b, 2)].reshape(2 * TILE, D), dpre, ((0,), (0,))).reshape(4, 64, D)
    grads[1] = dot(aggs[...].reshape(2 * TILE, D), dpre, ((0,), (0,))).reshape(4, 64, D)
    w.push("wc", grads.at[1 - core], s.grads_in, mate)
    bias_core = s.bias_core
    bias_core[0] = jnp.broadcast_to(jnp.sum(dpre.astype(F32), axis=0, keepdims=True), (8, D))
    w.push("vc", bias_core.at[0], bias_core.at[1], mate)
    for half in range(2):
        s.base[half] = dot(dpres[half], self_w[...], ((1,), (1,)))
    gather_step(2)
    weights_y()
    gather_step(3)
    gather_step(4)
    weights_x()
    w.take("x0", dagg(1 - xh, z, 0))
    for k in (1, 2, 3, 4):
        w.take("xu%d" % k, dagg(1 - xh, z_at(8 - k), 0, low if k == 4 else None))
        w.take("xd%d" % k, dagg(1 - xh, z_at(k), 0, high if k == 4 else None))

    core_out, core_in = s.core_out, s.core_in
    y0_out, y0_in, y1_out, y1_in = s.y0_out, s.y0_in, s.y1_out, s.y1_in
    groups = (((1, 2), (0, 2)), ((1, 1), (1, 3)), ((0, 1), (0, 3)), ((1, 0), (0, 0)))

    def column(k):
        return (xl, other)[k]

    def back(k, o, to_core):
        to = block(column(k), y_at(o), to_core)
        add_pairs(bwd, tiles, daggs, runs, 9 * to, 9, jnp.zeros((TILE, D), F32), True)

    def term(k, o, to_core, half):
        return runs[within(bwd_last[0, 2 * block(column(k), y_at(o), to_core) + half], PAIRS)]

    def for_mate(g):
        for j, (k, o) in enumerate(groups[g]):
            back(k, o, 1 - core)
        for j, (k, o) in enumerate(groups[g]):
            for half in range(2):
                core_out[g, j, half] = term(k, o, 1 - core, half).astype(BF)
            w.push("k%d%d" % (g, j), core_out.at[g, j], core_in.at[g, j], mate)

    def for_own(g):
        for k, o in groups[g]:
            back(k, o, core)

    def chip_term(g, j, half):
        k, o = groups[g][j]
        return term(k, o, core, half) + core_in[g, j, half].astype(F32)

    def opposite():
        for j in range(2):
            k = groups[0][j][0]
            w.take("k0%d" % j, core_in.at[0, j])
            for way, device in enumerate((y_up, y_down)):
                y0_out[way, k] = chip_term(0, j, way).astype(BF)
                w.push("p%d%d" % (way, k), y0_out.at[way, k], y0_in.at[way, k], device)

    def neighbours(g):
        k = groups[g][0][0]
        for way, device in enumerate((y_up, y_down)):
            w.take("k%d%d" % (g, way), core_in.at[g, way])
            y1_out[way, k, 1 - way] = chip_term(g, way, 1 - way).astype(BF)
            w.push("q%d%d%d" % (way, k, 1 - way), y1_out.at[way, k, 1 - way], y1_in.at[way, k, 1 - way], device)
        for way, device in enumerate((y_up, y_down)):
            w.take("p%d%d" % (way, k), y0_in.at[way, k])
            y1_out[way, k, way] = (chip_term(g, way, way) + y0_in[way, k].astype(F32)).astype(BF)
            w.push("q%d%d%d" % (way, k, way), y1_out.at[way, k, way], y1_in.at[way, k, way], device)

    def column_sum(j, half):
        k = groups[3][j][0]
        for way in range(2):
            w.take("q%d%d%d" % (way, k, half), y1_in.at[way, k, half])
        return chip_term(3, j, half) + y1_in[0, k, half].astype(F32) + y1_in[1, k, half].astype(F32)

    for_mate(0)
    for_mate(1)
    weights_z()
    for_own(0)
    opposite()
    for_mate(2)
    for_own(1)
    neighbours(1)
    weights_total()
    for_mate(3)
    for_own(2)
    neighbours(2)
    for_own(3)
    w.take("k30", core_in.at[3, 0])
    w.take("k31", core_in.at[3, 1])
    for half in range(2):
        s.x_out[half] = column_sum(0, half).astype(BF)
        w.push("x%d" % (half + 8), s.x_out.at[half], s.x_in.at[half], x_side)
    weights_back_core()
    for half in range(2):
        s.base[half] = s.base[half] + column_sum(1, half)
    for half in range(2):
        w.take("x%d" % (half + 8), s.x_in.at[half])
        grad_features[half * TILE:half * TILE + TILE] = (s.base[half] + s.x_in[half].astype(F32)).astype(BF)
    writes[1].start()
    w.take("tc", full.at[1 - core])
    writes[2].start()
    writes[3].start()
    for write in writes:
        write.wait()
    w.flush()
    assert len(w.names) <= WIRES


OUTPUTS = [jax.ShapeDtypeStruct((2 * TILE, D), BF)] * 2 + [jax.ShapeDtypeStruct((D, D), F32)] * 2 + [jax.ShapeDtypeStruct((D,), F32)]


def hand_over(*refs):
    for k in range(5):
        refs[5 + k][...] = refs[k][...]


def body(features, tiles, tile_rows, tile_cols, tile_counts, self_weight, neigh_weight, bias, out_grad):
    anywhere = pl.BlockSpec(memory_space=pl.ANY)
    made = pl.pallas_call(
        layer_kernel,
        out_shape=OUTPUTS,
        in_specs=[anywhere] * 9,
        out_specs=[anywhere] * 5,
        scratch_shapes=[pltpu.VMEM(*spec) for spec in SCRATCH.values()] + [
            pltpu.SMEM((8, 384), I32), pltpu.SMEM((8, 128), I32), pltpu.SMEM((8, 384), I32), pltpu.SMEM((8, 128), I32),
            pltpu.SemaphoreType.DMA((WIRES,)), pltpu.SemaphoreType.DMA((WIRES,)),
            pltpu.SemaphoreType.DMA, pltpu.SemaphoreType.DMA((4,)), pltpu.SemaphoreType.DMA((9,)), pltpu.SemaphoreType.DMA((5,)),
        ],
        compiler_params=pltpu.CompilerParams(collective_id=0, has_side_effects=True, vmem_limit_bytes=56 << 20),
        name="sage_layer",
    )(features, tiles.reshape(1, LIVE, TILE, TILE), tile_rows, tile_cols, tile_counts, self_weight, neigh_weight, bias, out_grad)
    return pl.pallas_call(
        hand_over,
        out_shape=OUTPUTS,
        in_specs=[pl.BlockSpec(memory_space=pltpu.VMEM)] * 5,
        out_specs=[pl.BlockSpec(memory_space=pltpu.VMEM)] * 5,
        name="hand_over",
    )(*made)


def solution(mesh):
    split = ("blk", "rep")
    return jax.shard_map(
        body,
        mesh=mesh,
        in_specs=(P(split, None), P(split, None, None, None, None), P(split, None, None), P(split, None, None), P(split, None),
                  P(), P(), P(), P(split, None)),
        out_specs=(P(split, None), P(split, None), P(), P(), P()),
        check_vma=False,
    )
```

```python
import types

import jax
import jax.numpy as jnp
from jax import lax
from jax.experimental import pallas as pl
from jax.experimental.pallas import tpu as pltpu
from jax.sharding import PartitionSpec as P

BF, F32, I32 = jnp.bfloat16, jnp.float32, jnp.int32
MESH = pl.DeviceIdType.MESH
N_SRC = 16
SLOTS = 16
LIVE = N_SRC * SLOTS
TILE = 128
D = 256
SEGMENTS = 32
PAIRS = (LIVE + SEGMENTS) // 2
DEAD = 40
FWD_STEP = 48


def iota(shape, dim):
    return lax.broadcasted_iota(I32, shape, dim)


def ones_where(cond):
    return jnp.where(cond, 1.0, 0.0).astype(BF)


def dot(a, b, contract=((1,), (0,))):
    return lax.dot_general(a, b, (contract, ((), ())), preferred_element_type=F32)


def spread(table):
    slot = iota((LIVE, SLOTS), 0)
    picked = dot(ones_where(slot // SLOTS == iota((LIVE, SLOTS), 1)), table.astype(F32).astype(BF))
    own = jnp.where(slot % SLOTS == iota((LIVE, SLOTS), 1), picked, 0.0).astype(BF)
    ones = jnp.ones((LIVE, SLOTS), BF)
    return dot(own, ones, ((1,), (1,))), dot(ones, own, ((1,), (1,)))


def pair_table(key, other, by_source):
    down, along = spread(key)
    _, other_along = spread(other)
    before = (down == along) & (iota((LIVE, LIVE), 1) < iota((LIVE, LIVE), 0))
    place_in = dot(ones_where(before), jnp.ones((LIVE, 128), BF))
    member = down[:, :128] == iota((LIVE, 128), 1).astype(F32)
    size = dot(jnp.ones((LIVE, LIVE), BF), ones_where(member))
    pairs = jnp.floor((size + 1.0) * 0.5)
    group, later = iota((128, 128), 0), iota((128, 128), 1)
    if by_source:
        first_pair = dot(pairs.astype(BF), ones_where((later % 2 == 1) & (group == later - 1)))
        first_pair = first_pair + (9 * (iota((LIVE, 128), 1) // 2)).astype(F32)
    else:
        first_pair = dot(pairs.astype(BF), ones_where(group < later))
    own_first = dot(jnp.where(member & (iota((LIVE, 128), 1) < SEGMENTS), first_pair, 0.0).astype(BF), jnp.ones((128, 128), BF))
    place = 2.0 * own_first + place_in
    place = jnp.where(down[:, :128] < float(SEGMENTS), place, -1.0)
    place3 = jnp.concatenate([place, place, place], axis=1)
    place_in3 = jnp.concatenate([place_in, place_in, place_in], axis=1)
    held = place3 == iota((LIVE, 384), 1).astype(F32)
    held_low = ones_where(held)
    slot = iota((8, LIVE), 1)
    which = dot((slot - LIVE).astype(F32).astype(BF), held_low) + float(LIVE)
    what = dot(other_along[0:8].astype(BF), held_low)
    opens = dot(jnp.ones((8, LIVE), BF), ones_where(held & (place_in3 == 0.0)))
    row = iota((8, 384), 0)
    table = jnp.where(row == 0, which, jnp.where(row == 1, what, opens)).astype(I32)
    last = jnp.where(size > 0.0, first_pair + pairs, 0.0)[0:8].astype(I32)
    return table, last


def make_tables(rows, cols, counts, forward, forward_last, backward, backward_last):
    diagonal = iota((N_SRC, SLOTS), 0) == iota((N_SRC, SLOTS), 1)
    counted = jnp.where(diagonal, counts.astype(F32), 0.0).astype(BF)
    live = iota((N_SRC, SLOTS), 1).astype(F32) < dot(counted, jnp.ones((N_SRC, SLOTS), BF))
    source = 2 * iota((N_SRC, SLOTS), 0) + cols
    table, last = pair_table(jnp.where(live, rows, DEAD), source, False)
    forward[...] = table
    forward_last[...] = last
    table, last = pair_table(jnp.where(live, source, DEAD), rows, True)
    backward[...] = table
    backward_last[...] = last


def within(index, top):
    return jnp.minimum(jnp.maximum(index, 0), top)


def add_pairs(table, tiles, values, runs, first, count, running, transposed):
    for step in range(count):
        p = first + step
        left, right = within(table[0, 2 * p], LIVE), within(table[0, 2 * p + 1], LIVE)
        pick, pick_right = within(table[1, 2 * p], SEGMENTS - 1), within(table[1, 2 * p + 1], SEGMENTS - 1)
        held = jnp.concatenate([values[pick], values[pick_right]], axis=0)
        if transposed:
            product = dot(jnp.concatenate([tiles[left], tiles[right]], axis=0), held, ((0,), (0,)))
        else:
            product = dot(jnp.concatenate([tiles[left], tiles[right]], axis=1), held)
        running = product + jnp.where(table[2, 2 * p] > 0, 0.0, running)
        runs[p + 1] = running


class Wires:
    def __init__(self, send_sem, recv_sem, anyone):
        self.send_sem, self.recv_sem, self.anyone = send_sem, recv_sem, anyone
        self.names, self.pending = {}, []

    def copy(self, name, source, target, device):
        k = self.names.setdefault(name, len(self.names))
        return pltpu.make_async_remote_copy(
            src_ref=source, dst_ref=target, send_sem=self.send_sem.at[k], recv_sem=self.recv_sem.at[k],
            device_id=device, device_id_type=MESH)

    def push(self, name, source, target, device):
        copy = self.copy(name, source, target, device)
        copy.start()
        self.pending.append(copy)

    def take(self, name, target):
        self.copy(name, target, target, self.anyone).wait_recv()

    def flush(self):
        for copy in self.pending:
            copy.wait_send()
        self.pending = []


SCRATCH = dict(
    tiles=((LIVE + 1, TILE, TILE), BF), feats=((32, TILE, D), BF), runs=((PAIRS + 1, TILE, D), F32),
    daggs=((32, TILE, D), BF),
    fwd_v=((8, 384), I32), fwd_last_v=((8, 128), I32), bwd_v=((8, 384), I32), bwd_last_v=((8, 128), I32),
    self_part=((2, TILE, D), F32), aggs=((2, TILE, D), BF), dpres=((2, TILE, D), BF), base=((2, TILE, D), F32),
    a_up_out=((4, 2, TILE, D), BF), a_up_in=((4, 2, TILE, D), BF), a_down_out=((4, 2, TILE, D), BF), a_down_in=((4, 2, TILE, D), BF),
    b_up_out=((4, TILE, D), BF), b_up_in=((4, TILE, D), BF), b_down_out=((4, TILE, D), BF), b_down_in=((4, TILE, D), BF),
    bx_out=((8, TILE, D), BF), bx_in=((8, TILE, D), BF), ax_out=((TILE, D), BF), ax_in=((TILE, D), BF), a_own=((TILE, D), F32),
    core_out=((4, 2, 2, TILE, D), BF), core_in=((4, 2, 2, TILE, D), BF),
    y0_out=((2, 2, TILE, D), BF), y0_in=((2, 2, TILE, D), BF), y1_out=((2, 2, 2, TILE, D), BF), y1_in=((2, 2, 2, TILE, D), BF),
    rows=((1, N_SRC, SLOTS), I32), cols=((1, N_SRC, SLOTS), I32), counts=((1, N_SRC), I32), self_w=((D, D), BF), neigh_w=((D, D), BF),
    bias=((D,), F32), out_grad=((2 * TILE, D), BF), output=((2 * TILE, D), BF), grad_features=((2 * TILE, D), BF), grad_bias=((D,), F32),
    x_out=((2, TILE, D), BF), x_in=((2, TILE, D), BF),
    grads=((2, 4, 64, D), F32), grads_in=((4, 64, D), F32), chip=((4, 72, D), F32), y_parts=((4, 72, D), F32), quarter=((4, 24, D), F32), x_parts=((4, 24, D), F32),
    z_parts=((8, 24, D), F32), full=((2, D, D), F32), bias_core=((2, 8, D), F32),
)
WIRES = 160


def layer_kernel(features, tiles_hbm, *rest):
    in_hbm, out_hbm, scratch = rest[:7], rest[7:12], rest[12:]
    s = types.SimpleNamespace(**dict(zip(SCRATCH, scratch)))
    fwd, fwd_last, bwd, bwd_last, send_sem, recv_sem, tile_sem, table_sem, in_sem, out_sem = scratch[len(SCRATCH):]
    tiles, feats, runs, daggs = s.tiles, s.feats, s.runs, s.daggs
    b, r = lax.axis_index("blk"), lax.axis_index("rep")
    xl, y, core = b // 8, lax.rem(b // 2, 4), lax.rem(b, 2)
    xh, z = r // 8, lax.rem(r, 8)
    x = 2 * xh + xl

    def block(xl, y, core):
        return xl * 8 + y * 2 + core

    def y_at(o):
        return lax.rem(y + o, 4)

    def z_at(o):
        return lax.rem(z + o, 8)

    def x_at(o):
        return lax.rem(x + o, 4)

    x_side, y_up, y_down, mate = (block(1 - xl, y, core), r), (block(xl, y_at(1), core), r), (block(xl, y_at(3), core), r), (block(xl, y, 1 - core), r)
    z_up, z_down, x_far = (b, xh * 8 + z_at(1)), (b, xh * 8 + z_at(7)), (b, (1 - xh) * 8 + z)
    turns = [(i, j) for i in range(4) for j in range(4) if i or j]
    plane = {(i, j): (block(lax.rem(x_at(i), 2), y_at(j), core), (x_at(i) // 2) * 8 + z) for i, j in turns}

    def plane_part(i, j):
        return 4 * y_at(j) + x_at(i)

    own_part = 4 * y + x
    z_peer = {o: (b, xh * 8 + z_at(o)) for o in range(1, 8)}
    w = Wires(send_sem, recv_sem, mate)

    load = pltpu.make_async_copy(tiles_hbm.at[0], tiles.at[pl.ds(0, LIVE)], tile_sem)
    held = (s.rows, s.cols, s.counts, s.self_w, s.neigh_w, s.bias, s.out_grad)
    reads = [pltpu.make_async_copy(features.at[pl.ds(half * TILE, TILE)], feats.at[2 * b + half], in_sem.at[half]) for half in range(2)]
    reads += [pltpu.make_async_copy(source, target, in_sem.at[2 + k]) for k, (source, target) in enumerate(zip(in_hbm, held))]
    barrier = pltpu.get_barrier_semaphore()
    partners = [mate, *plane.values(), *z_peer.values()]
    for partner in partners:
        pl.semaphore_signal(barrier, inc=1, device_id=partner, device_id_type=MESH)
    for read in reads:
        read.start()
    load.start()
    rows, cols, counts, self_w, neigh_w, bias, out_grad = held
    output, grad_features, full = s.output, s.grad_features, s.full
    made = (output, grad_features, full.at[0], full.at[1], s.grad_bias)
    writes = [pltpu.make_async_copy(source, target, out_sem.at[k]) for k, (source, target) in enumerate(zip(made, out_hbm))]
    tiles[LIVE] = jnp.zeros((TILE, TILE), BF)
    runs[0] = jnp.zeros((TILE, D), F32)
    pl.semaphore_wait(barrier, len(partners))

    def feat(xl, y, core, half):
        return feats.at[2 * block(xl, y, core) + half]

    mates = []

    def spread_feat(name, where, device):
        w.push(name, feat(*where), feat(*where), device)

    def to_mate(xl, y, half):
        spread_feat("m%d" % len(mates), (xl, y, core, half), mate)
        mates.append((xl, y, half))

    def arrived(name, xl, y, half):
        w.take(name, feat(xl, y, core, half))
        to_mate(xl, y, half)

    other, before, behind, across = 1 - xl, y_at(3), y_at(1), y_at(2)
    for half in range(2):
        here = features.at[pl.ds(half * TILE, TILE)]
        there = feat(xl, y, core, half)
        w.push("fx%d" % half, here, there, x_side)
        w.push("fu0%d" % half, here, there, y_up)
        w.push("fd0%d" % half, here, there, y_down)
        w.push("m%d" % half, here, there, mate)
        mates.append((xl, y, half))

    for read in reads:
        read.wait()
    arrived("fx0", other, y, 0)
    spread_feat("fu10", (other, y, core, 0), y_up)
    spread_feat("fd10", (other, y, core, 0), y_down)
    arrived("fu00", xl, before, 0)
    spread_feat("fu2", (xl, before, core, 0), y_up)
    arrived("fx1", other, y, 1)
    spread_feat("fu11", (other, y, core, 1), y_up)
    spread_feat("fd11", (other, y, core, 1), y_down)
    arrived("fd01", xl, behind, 1)
    spread_feat("fd2", (xl, behind, core, 1), y_down)
    arrived("fd00", xl, behind, 0)
    arrived("fu01", xl, before, 1)
    arrived("fu10", other, before, 0)
    spread_feat("fu3", (other, before, core, 0), y_up)
    arrived("fd10", other, behind, 0)
    arrived("fd11", other, behind, 1)
    spread_feat("fd3", (other, behind, core, 1), y_down)
    arrived("fu11", other, before, 1)
    arrived("fu2", xl, across, 0)
    arrived("fd2", xl, across, 1)
    make_tables(rows[0], cols[0], counts[...], s.fwd_v, s.fwd_last_v, s.bwd_v, s.bwd_last_v)
    tables = [(s.fwd_v, fwd), (s.fwd_last_v, fwd_last), (s.bwd_v, bwd), (s.bwd_last_v, bwd_last)]
    tables = [pltpu.make_async_copy(here, there, table_sem.at[k]) for k, (here, there) in enumerate(tables)]
    for copy in tables:
        copy.start()
    for half in range(2):
        s.self_part[half] = dot(feats[2 * b + half], self_w[...]) + bias[...].reshape(1, D)
    arrived("fu3", other, across, 0)
    arrived("fd3", other, across, 1)
    for k, (side, at, half) in enumerate(mates):
        w.take("m%d" % k, feat(side, at, 1 - core, half))

    for copy in tables:
        copy.wait()
    load.wait()

    @pl.loop(0, PAIRS // FWD_STEP)
    def _(k):
        add_pairs(fwd, tiles, feats, runs, FWD_STEP * k, FWD_STEP, runs[FWD_STEP * k], False)

    def part(xh, z, half):
        return runs[within(fwd_last[0, (xh * 8 + z) * 2 + half], PAIRS)]

    a_up_out, a_up_in, a_down_out, a_down_in = s.a_up_out, s.a_up_in, s.a_down_out, s.a_down_in
    b_up_out, b_up_in, b_down_out, b_down_in = s.b_up_out, s.b_up_in, s.b_down_out, s.b_down_in
    bx_out, bx_in = s.bx_out, s.bx_in
    a_up_out[0, 0] = part(0, z_at(4), 0).astype(BF)
    w.push("au00", a_up_out.at[0, 0], a_up_in.at[0, 0], z_up)
    a_down_out[0, 1] = part(1, z_at(4), 0).astype(BF)
    w.push("ad01", a_down_out.at[0, 1], a_down_in.at[0, 1], z_down)
    offsets = (4, 3, 5, 2, 6, 1, 7, 0)

    def bx_send(j):
        bx_out[j] = part(1 - xh, z_at(offsets[j]), 1).astype(BF)
        w.push("bx%d" % j, bx_out.at[j], bx_in.at[j], x_far)

    bx_send(0)
    bx_send(1)
    a_up_out[1, 1] = part(1, z_at(3), 0).astype(BF)
    w.push("au11", a_up_out.at[1, 1], a_up_in.at[1, 1], z_up)
    a_down_out[1, 0] = part(0, z_at(5), 0).astype(BF)
    w.push("ad10", a_down_out.at[1, 0], a_down_in.at[1, 0], z_down)
    for j in range(2, 8):
        bx_send(j)
    low, high = pl.ds(0, TILE // 2), pl.ds(TILE // 2, TILE // 2)

    def a_step(k):
        for turn in ((0,) if k == 1 else (1, 0)):
            for name, out, into, device, o, half in (("au", a_up_out, a_up_in, z_up, 4 - k, 0), ("ad", a_down_out, a_down_in, z_down, 4 + k, 1)):
                side = half if turn == 0 else 1 - half
                w.take("%s%d%d" % (name, k - 1, side), into.at[k - 1, side])
                out[k, side] = (part(side, z_at(o), 0) + into[k - 1, side].astype(F32)).astype(BF)
                w.push("%s%d%d" % (name, k, side), out.at[k, side], into.at[k, side], device)

    def b_step(k):
        if k == 0:
            w.take("bx0", bx_in.at[0])
            value = (part(xh, z_at(4), 1) + bx_in[0].astype(F32)).astype(BF)
            b_up_out[0] = value
            b_down_out[0] = value
            w.push("bu0", b_up_out.at[0, low], b_up_in.at[0, low], z_up)
            w.push("bd0", b_down_out.at[0, high], b_down_in.at[0, high], z_down)
            return
        for name, out, into, device, j, rows_in in (("bu", b_up_out, b_up_in, z_up, 2 * k - 1, low), ("bd", b_down_out, b_down_in, z_down, 2 * k, high)):
            w.take("bx%d" % j, bx_in.at[j])
            w.take("%s%d" % (name, k - 1), into.at[0, rows_in] if k == 1 else into.at[k - 1])
            value = part(xh, z_at(offsets[j]), 1) + bx_in[j].astype(F32)
            if k > 1:
                value = value + into[k - 1].astype(F32)
            elif name == "bu":
                value = jnp.concatenate([value[:TILE // 2] + into[0, :TILE // 2].astype(F32), value[TILE // 2:]], axis=0)
            else:
                value = jnp.concatenate([value[:TILE // 2], value[TILE // 2:] + into[0, TILE // 2:].astype(F32)], axis=0)
            out[k] = value.astype(BF)
            w.push("%s%d" % (name, k), out.at[k], into.at[k], device)

    for k in (1, 2, 3):
        a_step(k)
        b_step(k - 1)
    for side in range(2):
        w.take("au3%d" % side, a_up_in.at[3, side])
        w.take("ad3%d" % side, a_down_in.at[3, side])

    def a_sum(side):
        return part(side, z, 0) + a_up_in[3, side].astype(F32) + a_down_in[3, side].astype(F32)

    s.ax_out[...] = a_sum(1 - xh).astype(BF)
    w.push("ax", s.ax_out, s.ax_in, x_far)
    b_step(3)
    s.a_own[...] = a_sum(xh)

    def layer(half, aggregate):
        here = slice(half * TILE, half * TILE + TILE)
        low_agg = aggregate.astype(BF)
        s.aggs[half] = low_agg
        preact = s.self_part[half] + dot(low_agg, neigh_w[...])
        gate = jax.nn.sigmoid(preact)
        output[here] = (preact * gate).astype(BF)
        dpre = (out_grad[here].astype(F32) * gate * (1.0 + preact * (1.0 - gate))).astype(BF)
        s.dpres[half] = dpre
        daggs[2 * r + half] = dot(dpre, neigh_w[...], ((1,), (1,))).astype(BF)

    def dagg(xh, z, half, rows=None):
        at = (xh * 8 + z) * 2 + half
        return daggs.at[at] if rows is None else daggs.at[at, rows]

    def spread_dagg(name, where, device, rows=None):
        w.push(name, dagg(*where, rows), dagg(*where, rows), device)

    w.take("ax", s.ax_in)
    layer(0, s.a_own[...] + s.ax_in[...].astype(F32))
    spread_dagg("gu1", (xh, z, 0), z_up)
    spread_dagg("gd1", (xh, z, 0), z_down)
    spread_dagg("x0", (xh, z, 0), x_far)
    w.take("bx7", bx_in.at[7])
    w.take("bu3", b_up_in.at[3])
    w.take("bd3", b_down_in.at[3])
    layer(1, part(xh, z, 1) + bx_in[7].astype(F32) + b_up_in[3].astype(F32) + b_down_in[3].astype(F32))
    spread_dagg("gx", (xh, z, 1), x_far)
    spread_dagg("hu1", (xh, z, 1), z_up)
    spread_dagg("hd1", (xh, z, 1), z_down)

    writes[0].start()
    aggs, dpres, grads = s.aggs, s.dpres, s.grads
    w.take("gx", dagg(1 - xh, z, 1))
    spread_dagg("iu1", (1 - xh, z, 1), z_up)
    spread_dagg("id1", (1 - xh, z, 1), z_down)

    def gather_step(k):
        for name, side, half in (("g", xh, 0), ("h", xh, 1), ("i", 1 - xh, 1)):
            for way, device, o, rows in (("u", z_up, 8 - k, low), ("d", z_down, k, high)):
                rows_in = rows if k == 4 else None
                w.take("%s%s%d" % (name, way, k), dagg(side, z_at(o), half, rows_in))
                if k < 4:
                    spread_dagg("%s%s%d" % (name, way, k + 1), (side, z_at(o), half), device, rows if k == 3 else None)
                if half == 0:
                    spread_dagg("x%s%d" % (way, k), (side, z_at(o), half), x_far, rows_in)

    chip, y_parts, quarter, x_parts, z_parts = s.chip, s.y_parts, s.quarter, s.x_parts, s.z_parts

    def weights_y():
        w.take("wc", s.grads_in)
        w.take("vc", bias_core.at[1])
        chip[:, 0:64] = grads[core] + s.grads_in[...]
        chip[:, 64:72] = jnp.broadcast_to((bias_core[0] + bias_core[1])[None], (4, 8, D))
        y_parts[y] = chip[y]
        for o in (1, 2, 3):
            w.push("wy%d" % o, chip.at[y_at(o)], y_parts.at[y], plane[0, o])

    def weights_x():
        for o in (1, 2, 3):
            w.take("wy%d" % o, y_parts.at[y_at(4 - o)])
        total = (y_parts[0] + y_parts[1]) + (y_parts[2] + y_parts[3])
        quarter[:, 0:16] = total[0:64].reshape(4, 16, D)
        quarter[:, 16:24] = jnp.broadcast_to(total[64:72][None], (4, 8, D))
        x_parts[x] = quarter[x]
        for o in (1, 2, 3):
            w.push("wx%d" % o, quarter.at[x_at(o)], x_parts.at[x], plane[o, 0])

    def weights_z():
        for o in (1, 2, 3):
            w.take("wx%d" % o, x_parts.at[x_at(4 - o)])
        total = (x_parts[0] + x_parts[1]) + (x_parts[2] + x_parts[3])
        z_parts[z] = total
        for o in range(1, 8):
            w.push("wz%d" % o, z_parts.at[z], z_parts.at[z], z_peer[o])

    def rows_of(part):
        return full.at[core, pl.ds(16 * part, 16)]

    def weights_total():
        for o in range(1, 8):
            w.take("wz%d" % o, z_parts.at[z_at(8 - o)])
        total = z_parts[0]
        for o in range(1, 8):
            total = total + z_parts[o]
        full[core, pl.ds(16 * own_part, 16)] = total[0:16]
        s.grad_bias[...] = total[16]
        writes[4].start()
        for i, j in turns:
            w.push("t%d%d" % (i, j), rows_of(own_part), rows_of(own_part), plane[i, j])

    def weights_back_core():
        for i, j in turns:
            w.take("t%d%d" % (i, j), rows_of(plane_part(4 - i, 4 - j)))
        w.push("tc", full.at[core], full.at[core], mate)

    gather_step(1)
    dpre = dpres[...].reshape(2 * TILE, D)
    grads[0] = dot(feats[pl.ds(2 * b, 2)].reshape(2 * TILE, D), dpre, ((0,), (0,))).reshape(4, 64, D)
    grads[1] = dot(aggs[...].reshape(2 * TILE, D), dpre, ((0,), (0,))).reshape(4, 64, D)
    w.push("wc", grads.at[1 - core], s.grads_in, mate)
    bias_core = s.bias_core
    bias_core[0] = jnp.broadcast_to(jnp.sum(dpre.astype(F32), axis=0, keepdims=True), (8, D))
    w.push("vc", bias_core.at[0], bias_core.at[1], mate)
    for half in range(2):
        s.base[half] = dot(dpres[half], self_w[...], ((1,), (1,)))
    gather_step(2)
    weights_y()
    gather_step(3)
    gather_step(4)
    weights_x()
    w.take("x0", dagg(1 - xh, z, 0))
    for k in (1, 2, 3, 4):
        w.take("xu%d" % k, dagg(1 - xh, z_at(8 - k), 0, low if k == 4 else None))
        w.take("xd%d" % k, dagg(1 - xh, z_at(k), 0, high if k == 4 else None))

    core_out, core_in = s.core_out, s.core_in
    y0_out, y0_in, y1_out, y1_in = s.y0_out, s.y0_in, s.y1_out, s.y1_in
    groups = (((1, 2), (0, 2)), ((1, 1), (1, 3)), ((0, 1), (0, 3)), ((1, 0), (0, 0)))

    def column(k):
        return (xl, other)[k]

    def back(k, o, to_core):
        to = block(column(k), y_at(o), to_core)
        add_pairs(bwd, tiles, daggs, runs, 9 * to, 9, jnp.zeros((TILE, D), F32), True)

    def term(k, o, to_core, half):
        return runs[within(bwd_last[0, 2 * block(column(k), y_at(o), to_core) + half], PAIRS)]

    def for_mate(g):
        for j, (k, o) in enumerate(groups[g]):
            back(k, o, 1 - core)
        for j, (k, o) in enumerate(groups[g]):
            for half in range(2):
                core_out[g, j, half] = term(k, o, 1 - core, half).astype(BF)
            w.push("k%d%d" % (g, j), core_out.at[g, j], core_in.at[g, j], mate)

    def for_own(g):
        for k, o in groups[g]:
            back(k, o, core)

    def chip_term(g, j, half):
        k, o = groups[g][j]
        return term(k, o, core, half) + core_in[g, j, half].astype(F32)

    def opposite():
        for j in range(2):
            k = groups[0][j][0]
            w.take("k0%d" % j, core_in.at[0, j])
            for way, device in enumerate((y_up, y_down)):
                y0_out[way, k] = chip_term(0, j, way).astype(BF)
                w.push("p%d%d" % (way, k), y0_out.at[way, k], y0_in.at[way, k], device)

    def near(g):
        k = groups[g][0][0]
        for way, device in enumerate((y_up, y_down)):
            w.take("k%d%d" % (g, way), core_in.at[g, way])
            y1_out[way, k, 1 - way] = chip_term(g, way, 1 - way).astype(BF)
            w.push("q%d%d%d" % (way, k, 1 - way), y1_out.at[way, k, 1 - way], y1_in.at[way, k, 1 - way], device)

    def late(g):
        k = groups[g][0][0]
        for way, device in enumerate((y_up, y_down)):
            w.take("p%d%d" % (way, k), y0_in.at[way, k])
            y1_out[way, k, way] = (chip_term(g, way, way) + y0_in[way, k].astype(F32)).astype(BF)
            w.push("q%d%d%d" % (way, k, way), y1_out.at[way, k, way], y1_in.at[way, k, way], device)

    def column_sum(j, half):
        k = groups[3][j][0]
        for way in range(2):
            w.take("q%d%d%d" % (way, k, half), y1_in.at[way, k, half])
        return chip_term(3, j, half) + y1_in[0, k, half].astype(F32) + y1_in[1, k, half].astype(F32)

    for_mate(0)
    for_mate(1)
    weights_z()
    for_own(0)
    opposite()
    for_mate(2)
    for_own(1)
    near(1)
    for_mate(3)
    for_own(2)
    near(2)
    late(1)
    weights_total()
    for_own(3)
    late(2)
    w.take("k30", core_in.at[3, 0])
    w.take("k31", core_in.at[3, 1])
    for half in range(2):
        s.x_out[half] = column_sum(0, half).astype(BF)
        w.push("x%d" % (half + 8), s.x_out.at[half], s.x_in.at[half], x_side)
    weights_back_core()
    for half in range(2):
        s.base[half] = s.base[half] + column_sum(1, half)
    for half in range(2):
        w.take("x%d" % (half + 8), s.x_in.at[half])
        grad_features[half * TILE:half * TILE + TILE] = (s.base[half] + s.x_in[half].astype(F32)).astype(BF)
    writes[1].start()
    w.take("tc", full.at[1 - core])
    writes[2].start()
    writes[3].start()
    for write in writes:
        write.wait()
    w.flush()
    assert len(w.names) <= WIRES


OUTPUTS = [jax.ShapeDtypeStruct((2 * TILE, D), BF)] * 2 + [jax.ShapeDtypeStruct((D, D), F32)] * 2 + [jax.ShapeDtypeStruct((D,), F32)]


def hand_over(*refs):
    for k in range(5):
        refs[5 + k][...] = refs[k][...]


def body(features, tiles, tile_rows, tile_cols, tile_counts, self_weight, neigh_weight, bias, out_grad):
    anywhere = pl.BlockSpec(memory_space=pl.ANY)
    made = pl.pallas_call(
        layer_kernel,
        out_shape=OUTPUTS,
        in_specs=[anywhere] * 9,
        out_specs=[anywhere] * 5,
        scratch_shapes=[pltpu.VMEM(*spec) for spec in SCRATCH.values()] + [
            pltpu.SMEM((8, 384), I32), pltpu.SMEM((8, 128), I32), pltpu.SMEM((8, 384), I32), pltpu.SMEM((8, 128), I32),
            pltpu.SemaphoreType.DMA((WIRES,)), pltpu.SemaphoreType.DMA((WIRES,)),
            pltpu.SemaphoreType.DMA, pltpu.SemaphoreType.DMA((4,)), pltpu.SemaphoreType.DMA((9,)), pltpu.SemaphoreType.DMA((5,)),
        ],
        compiler_params=pltpu.CompilerParams(collective_id=0, has_side_effects=True, vmem_limit_bytes=56 << 20),
        name="sage_layer",
    )(features, tiles.reshape(1, LIVE, TILE, TILE), tile_rows, tile_cols, tile_counts, self_weight, neigh_weight, bias, out_grad)
    return pl.pallas_call(
        hand_over,
        out_shape=OUTPUTS,
        in_specs=[pl.BlockSpec(memory_space=pltpu.VMEM)] * 5,
        out_specs=[pl.BlockSpec(memory_space=pltpu.VMEM)] * 5,
        name="hand_over",
    )(*made)


def solution(mesh):
    split = ("blk", "rep")
    return jax.shard_map(
        body,
        mesh=mesh,
        in_specs=(P(split, None), P(split, None, None, None, None), P(split, None, None), P(split, None, None), P(split, None),
                  P(), P(), P(), P(split, None)),
        out_specs=(P(split, None), P(split, None), P(), P(), P()),
        check_vma=False,
    )
```
